32 devices in a mesh: tm: 16 (over z, x, core), panel: 2 (over y).
Axes of the slice: x: 2, y: 2, z: 4, core: 2. Of those that a mesh axis runs over, the one named last changes fastest.
Arguments:
- observations: bfloat16 [4096, 8192], P('panel', 'tm'), may hold values from -6 to 6
- info_weight: bfloat16 [4096, 1024], P('panel'), may hold values from -0.09375 to 0.09375
- readout: bfloat16 [4096, 1024], P('panel'), may hold values from -0.1875 to 0.1875
- labels: int32 [8192], P('tm'), may hold values from 0 to 3
- rate: float32 [4, 512], P(None, 'panel'), as said below
- angle: float32 [4, 512], P(None, 'panel'), may hold values from -0.3 to 0.3
- gain: float32 [4, 512], P(None, 'panel'), may hold values from 0.5 to 2
Outputs:
- smoothed: float32 [1024, 8192], P('panel', 'tm')
- predicted: bfloat16 [4096, 8192], P('panel', 'tm')
The draws below stay inside these ranges and needn't reach their ends.
Inputs may be any that keep to these rules, and one draw needn't show every extreme that they name: `rate`: every entry is positive.
All inputs are finite; a program needn't handle non-finite values.
Results may differ from the reference program's by a relative error of at most 0.013.
Values may be sent and summed in bfloat16 or wider, within the bound.
A program may use at most 128 MiB of HBM per device.

```python
import math
import jax
import jax.numpy as jnp
from jax import lax

REGION_LATENT = 128
CORTICAL_REGIONS = 8
UNITS = 4096
SWITCH_STATES = 4
INTERVAL_WIDTH = 512
LATENTS = 1024
PAIRS = 512
TEMPORAL_LENGTH = 8192


def draw_labels(key, part):
    leading_entry, trailing_segment, forced_key = jax.random.split(jax.random.fold_in(key, 11), 3)
    minimum_intensity = jax.random.randint(leading_entry, (TEMPORAL_LENGTH,), 0, SWITCH_STATES - 1)
    activation_jump = jax.random.randint(trailing_segment, (TEMPORAL_LENGTH,), 0, 32 * INTERVAL_WIDTH) == 0
    forced_bin = jax.random.randint(forced_key, (), 0, TEMPORAL_LENGTH)
    activation_jump = jnp.logical_or(activation_jump, jnp.arange(TEMPORAL_LENGTH) == forced_bin)
    return jnp.where(activation_jump, SWITCH_STATES - 1, minimum_intensity).astype(jnp.int32)


def draw_rate(key, part):
    generator_tokens = jax.random.split(jax.random.fold_in(key, 23), 4)
    neural_counts = REGION_LATENT * CORTICAL_REGIONS // 2
    fraction_value = 0.5
    deviation_scale = jnp.exp(jax.random.uniform(generator_tokens[1], (SWITCH_STATES - 1, neural_counts), jnp.float32, jnp.log(0.3), jnp.log(1.5)))
    sluggish_factor = jax.random.uniform(generator_tokens[0], (neural_counts,), jnp.float32) < fraction_value
    decay_constant = jax.random.uniform(generator_tokens[2], (SWITCH_STATES - 1, neural_counts), jnp.float32, 8.0, 24.0)
    noise_variate = jnp.where(sluggish_factor[None, :], deviation_scale / TEMPORAL_LENGTH, 1.0 / decay_constant)
    activation_jump = jax.random.uniform(generator_tokens[3], (1, neural_counts), jnp.float32, 0.22, 0.7)
    return jnp.concatenate([noise_variate, activation_jump], 0).astype(jnp.float32)


def shard_levels(stream_key, shape, cuts, least, largest):
    level, own = 1.0, jax.random.fold_in(stream_key, 6)
    for dim, shards_of in cuts:
        draws = jnp.exp(jax.random.uniform(jax.random.fold_in(own, dim), (shards_of,), jnp.float32, least / len(cuts), largest / len(cuts)))
        level = level * jnp.repeat(draws, shape[dim] // shards_of).reshape([-1 if axis == dim else 1 for axis in range(len(shape))])
    return level


def noise(stream_key, extent, deviation, bound, cuts=(), kind=jnp.bfloat16):
    result = jax.random.normal(stream_key, extent, jnp.float32) * deviation
    if len(cuts) > 0:
        result = shard_levels(stream_key, extent, cuts, -0.22, 0.18) * result
    return jnp.clip(result, min=-bound, max=bound).astype(kind)


def setup_inputs(seed: int = 0) -> dict:
    seeds = jax.random.split(jax.random.key(seed), 8)
    observations = noise(seeds[0], (UNITS, TEMPORAL_LENGTH), 1.0, 6.0, ((0, 2), (1, 16)))
    info_weight = noise(seeds[1], (UNITS, LATENTS), UNITS ** -0.5, 0.09375, ((0, 2),))
    readout = noise(seeds[2], (UNITS, LATENTS), LATENTS ** -0.5, 0.1875, ((0, 2),))
    labels = draw_labels(jax.random.fold_in(seeds[7], 71), 0)
    rate = draw_rate(jax.random.fold_in(seeds[7], 71), 0)
    angle = jnp.clip(jax.random.uniform(seeds[5], (SWITCH_STATES, PAIRS), jnp.float32, -0.3, 0.3) * shard_levels(seeds[5], (SWITCH_STATES, PAIRS), ((1, 2),), -0.4, 0.0), -0.3, 0.3)
    gain = jnp.clip(jnp.exp(math.log(2.0) - 1.3862944 * jax.random.uniform(seeds[6], (SWITCH_STATES, PAIRS), jnp.float32) ** shard_levels(seeds[6], (SWITCH_STATES, PAIRS), ((1, 2),), -0.2, 0.2)), 0.5, 2.0)
    return {"observations": observations, "info_weight": info_weight, "readout": readout, "labels": labels, "rate": rate, "angle": angle, "gain": gain}


def step_map(state, items):
    sre, sim = state
    are, aim, ure, uim = items
    nre = are * sre - aim * sim + ure
    nim = are * sim + aim * sre + uim
    return ((nre, nim), (nre, nim))

def reference(observations, info_weight, readout, labels, rate, angle, gain):
    half = REGION_LATENT // 2
    info = jnp.dot(info_weight.T, observations, preferred_element_type=jnp.float32)
    view = info.reshape(CORTICAL_REGIONS, 2, half, TEMPORAL_LENGTH)
    zre = view[:, 0].reshape(CORTICAL_REGIONS * half, TEMPORAL_LENGTH).T
    zim = view[:, 1].reshape(CORTICAL_REGIONS * half, TEMPORAL_LENGTH).T
    lam = rate[labels]
    ang = angle[labels]
    scale = gain[labels] * jnp.sqrt(-jnp.expm1(-2.0 * lam))
    mag = jnp.exp(-lam)
    are = mag * jnp.cos(ang)
    aim = mag * jnp.sin(ang)
    zero = jnp.zeros_like(zre[0])
    _, (mre, mim) = lax.scan(step_map, (zero, zero), (are, aim, scale * zre, scale * zim))
    following = jnp.concatenate([labels[1:], labels[:1] * 0])
    lam_next = rate[following]
    ang_next = angle[following]
    mag_next = jnp.exp(-lam_next)
    final = (jnp.arange(TEMPORAL_LENGTH) == TEMPORAL_LENGTH - 1)[:, None]
    gre = jnp.where(final, 0.0, mag_next * jnp.cos(ang_next))
    gim = jnp.where(final, 0.0, -(mag_next * jnp.sin(ang_next)))
    coef = jnp.where(final, 1.0, -jnp.expm1(-2.0 * lam_next))
    _, (sre, sim) = lax.scan(step_map, (zero, zero), (gre, gim, coef * mre, coef * mim), reverse=True)
    smoothed = jnp.stack([sre.T.reshape(CORTICAL_REGIONS, half, TEMPORAL_LENGTH), sim.T.reshape(CORTICAL_REGIONS, half, TEMPORAL_LENGTH)], 1).reshape(CORTICAL_REGIONS * REGION_LATENT, TEMPORAL_LENGTH)
    smoothed_half = smoothed.astype(jnp.bfloat16)
    predicted = jnp.dot(readout, smoothed_half, preferred_element_type=jnp.float32).astype(jnp.bfloat16)
    return (smoothed, predicted)
```

```python
import functools

import jax
import jax.numpy as jnp
from jax import lax
from jax.experimental import pallas as pl
from jax.experimental.pallas import tpu as pltpu
from jax.sharding import PartitionSpec as P

LANES = 128
HALF = 64
CHUNKS = 8
ROWS = 16
MESH = pl.DeviceIdType.MESH


def mul(x, y):
    return x[0] * y[0] - x[1] * y[1], x[0] * y[1] + x[1] * y[0]


def cmul(x, y):
    return x[0] * y[0] + x[1] * y[1], x[0] * y[1] - x[1] * y[0]


def add(x, y):
    return x[0] + y[0], x[1] + y[1]


def smooth_kernel(
    n, pn, groups, gw, regimes,
    obs_hbm, w_hbm, lab_ref, tab_ref,
    sm_hbm, sh_hbm,
    obs, obs_t, w, own, rs_out, rs_in, xre, xim, are, aim, coef, mre, mim, pre, pim,
    chunk, msgs, enter, bound, smv, shv,
    in_sem, rs_send, rs_recv, cm_send, cm_recv, ag_send, ag_recv, out_sem,
):
    me = lax.axis_index("tm")
    mp = lax.axis_index("panel")
    units, bins = obs.shape
    lat = own.shape[1]
    steps = bins // CHUNKS
    wide = gw == 2 * LANES

    def panel(s):
        return lax.rem(mp + s, pn)

    obs_copy = pltpu.make_async_copy(obs_hbm, obs, in_sem.at[0])
    obs_copy.start()
    w_copies = {}
    for s in list(range(1, pn)) + [0]:
        columns = pl.ds(pl.multiple_of(panel(s) * lat, LANES), lat)
        w_copies[s] = pltpu.make_async_copy(w_hbm.at[:, columns], w.at[s], in_sem.at[1 + s])
        w_copies[s].start()

    barrier = pltpu.get_barrier_semaphore()

    for s in range(1, pn):
        pl.semaphore_signal(barrier, inc=1, device_id=(me, panel(s)), device_id_type=MESH)

    def greet(s, _):
        pl.semaphore_signal(
            barrier, inc=1, device_id=(lax.rem(me + s, n), mp), device_id_type=MESH
        )
        return 0

    lax.fori_loop(1, n, greet, 0)

    obs_copy.wait()
    tile = 256

    def turn(i, _):
        rows = pl.ds(pl.multiple_of(i * tile, tile), tile)
        obs_t[:, rows] = obs[rows, :].T
        return 0

    lax.fori_loop(0, units // tile, turn, 0)

    def rs_copy(g, s):
        return pltpu.make_async_remote_copy(
            src_ref=rs_out.at[g, s - 1], dst_ref=rs_in.at[g, s - 1],
            send_sem=rs_send.at[g, s - 1], recv_sem=rs_recv.at[g, s - 1],
            device_id=(me, panel(s)), device_id_type=MESH,
        )

    def project(g, s):
        return jnp.dot(
            obs_t[...], w[s, :, g * gw:(g + 1) * gw], preferred_element_type=jnp.float32
        )

    for s in range(1, pn):
        w_copies[s].wait()
    for g in range(groups):
        for s in range(1, pn):
            rs_out[g, s - 1] = project(g, s).astype(jnp.bfloat16)
            if g == 0 and s == 1:
                pl.semaphore_wait(barrier, n - 1 + pn - 1)
            rs_copy(g, s).start()
    w_copies[0].wait()
    for g in range(groups):
        own[:, g * gw:(g + 1) * gw] = project(g, 0)

    lane = lax.broadcasted_iota(jnp.int32, (bins, LANES), 1)
    low = lane < HALF

    def swap(x):
        return pltpu.roll(x, HALF, 1)

    def gather_info(g):
        for s in range(1, pn):
            rs_copy(g, s).wait_recv()
        parts = []
        for h in range(gw // LANES):
            x = own[:, g * gw + h * LANES:g * gw + (h + 1) * LANES]
            for s in range(1, pn):
                x = x + rs_in[g, s - 1, :, h * LANES:(h + 1) * LANES].astype(jnp.float32)
            parts.append(x)
        if wide:
            xre[g] = jnp.where(low, parts[0], swap(parts[1]))
            xim[g] = jnp.where(low, swap(parts[0]), parts[1])
        else:
            xre[g] = parts[0]
            xim[g] = swap(parts[0])

    def rows_of(k):
        return pl.ds(pl.multiple_of(k * CHUNKS, CHUNKS), CHUNKS)

    def forward(g):
        def row(q, r):
            return jnp.broadcast_to(
                tab_ref[q * regimes + r:q * regimes + r + 1, g * LANES:(g + 1) * LANES],
                (CHUNKS, LANES),
            )

        table = [[row(q, r) for r in range(regimes)] for q in range(4)]

        def step(k, carry):
            m, p = carry
            rows = rows_of(k)
            label = lab_ref[rows, :]
            which = [label == r for r in range(regimes)]

            def pick(q):
                value = table[q][0]
                for r in range(1, regimes):
                    value = jnp.where(which[r], table[q][r], value)
                return value

            a = (pick(0), pick(1))
            scale, c = pick(2), pick(3)
            bin_rows = pl.ds(k, CHUNKS, stride=steps)
            u = (scale * xre[g, bin_rows, :], scale * xim[g, bin_rows, :])
            m = add(mul(a, m), u)
            p = mul(a, p)
            are[g, rows, :], aim[g, rows, :], coef[g, rows, :] = a[0], a[1], c
            mre[g, rows, :], mim[g, rows, :] = m
            pre[g, rows, :], pim[g, rows, :] = p
            return m, p

        zero = jnp.zeros((CHUNKS, LANES), jnp.float32)
        one = jnp.ones((CHUNKS, LANES), jnp.float32)
        return lax.fori_loop(0, steps, step, ((zero, zero), (one, zero)), unroll=4)

    def backward(g):
        def step(i, carry):
            e, d, w_ = carry
            k = steps - 2 - i
            rows, after = rows_of(k), rows_of(k + 1)
            a = (are[g, after, :], aim[g, after, :])
            c = coef[g, after, :]
            e = add(cmul(a, e), (c * mre[g, rows, :], c * mim[g, rows, :]))
            d = add(cmul(a, d), (c * pre[g, rows, :], c * pim[g, rows, :]))
            return e, d, cmul(a, w_)

        zero = jnp.zeros((CHUNKS, LANES), jnp.float32)
        one = jnp.ones((CHUNKS, LANES), jnp.float32)
        return lax.fori_loop(
            0, steps - 1, step, ((zero, zero), (zero, zero), (one, zero)), unroll=3
        )

    def chunk_row(g, q, c):
        return chunk[g, q, c:c + 1, :]

    def chunk_map(g, c):
        v = [chunk_row(g, q, c) for q in range(13)]
        return (v[0], v[1]), (v[2], v[3]), (v[4], v[5]), (v[6], v[7]), (v[8], v[9]), (v[10], v[11]), v[12]

    def local_map(g):
        b, a = forward(g)
        e, d, w_ = backward(g)
        first = rows_of(0)
        parts = (*a, *b, *w_, *e, *d, are[g, first, :], aim[g, first, :], coef[g, first, :])
        for q in range(13):
            chunk[g, q] = parts[q]
        A, B, G, E, D, a0, c0 = chunk_map(g, 0)
        for c in range(1, CHUNKS):
            Ar, Br, Gr, Er, Dr, ar, cr = chunk_map(g, c)
            K = cmul(ar, Dr)
            K = (K[0] + cr, K[1])
            E = add(E, mul(G, add(cmul(ar, Er), mul(K, B))))
            D = add(D, mul(G, mul(K, A)))
            G = mul(G, cmul(ar, Gr))
            A, B = mul(Ar, A), add(mul(Ar, B), Br)
        rows = (*A, *B, *G, *E, *D, *a0, c0)
        for q in range(13):
            msgs[g, 0, q:q + 1, :] = rows[q]
        msgs[g, 0, 13:ROWS, :] = jnp.zeros((ROWS - 13, LANES), jnp.float32)

    def cm_copy(g, s):
        return pltpu.make_async_remote_copy(
            src_ref=msgs.at[g, 0], dst_ref=msgs.at[g, s],
            send_sem=cm_send.at[g, s], recv_sem=cm_recv.at[g, s],
            device_id=(lax.rem(me + s, n), mp), device_id_type=MESH,
        )

    def each_peer(act):
        def go(s, _):
            act(s)
            return 0

        lax.fori_loop(1, n, go, 0)

    def boundary(g):
        zero = jnp.zeros((1, LANES), jnp.float32)

        def pair(slot, q):
            return msgs[g, slot, q:q + 1, :], msgs[g, slot, q + 1:q + 2, :]

        def put(d, row, value):
            enter[g, d, row:row + 1, :], enter[g, d, row + 1:row + 2, :] = value

        def get(d, row):
            return enter[g, d, row:row + 1, :], enter[g, d, row + 1:row + 2, :]

        def ahead(d, m):
            slot = lax.rem(me - d + n, n)
            put(d, 0, m)
            return add(mul(pair(slot, 0), m), pair(slot, 2))

        last = lax.fori_loop(0, n, ahead, (zero, zero))

        def back(i, s):
            d = n - 1 - i
            slot = lax.rem(me - d + n, n)
            put(d, 2, s)
            m = get(d, 0)
            first = add(add(mul(pair(slot, 4), s), pair(slot, 6)), mul(pair(slot, 8), m))
            c = msgs[g, slot, 12:13, :]
            return add(cmul(pair(slot, 10), first), (c * m[0], c * m[1]))

        lax.fori_loop(0, n, back, last)
        m_in, s_in = get(me, 0), get(me, 2)
        return m_in, s_in

    def finish(g):
        m, s = boundary(g)
        entering = []
        for c in range(CHUNKS):
            entering.append(m)
            bound[g, 0, c:c + 1, :], bound[g, 1, c:c + 1, :] = m
            A, B = chunk_map(g, c)[:2]
            m = add(mul(A, m), B)
        for c in reversed(range(CHUNKS)):
            bound[g, 2, c:c + 1, :], bound[g, 3, c:c + 1, :] = s
            _, _, G, E, D, a0, c0 = chunk_map(g, c)
            m = entering[c]
            first = add(add(mul(G, s), E), mul(D, m))
            s = add(cmul(a0, first), (c0 * m[0], c0 * m[1]))
        m_in = (bound[g, 0], bound[g, 1])
        s_in = (bound[g, 2], bound[g, 3])
        end = pl.ds(steps - 1, CHUNKS, stride=steps)
        xre[g, end, :], xim[g, end, :] = s_in

        def step(i, s):
            k = steps - 2 - i
            rows, after = rows_of(k), rows_of(k + 1)
            a = (are[g, after, :], aim[g, after, :])
            c = coef[g, after, :]
            m = add((mre[g, rows, :], mim[g, rows, :]), mul((pre[g, rows, :], pim[g, rows, :]), m_in))
            s = add(cmul(a, s), (c * m[0], c * m[1]))
            bin_rows = pl.ds(k, CHUNKS, stride=steps)
            xre[g, bin_rows, :], xim[g, bin_rows, :] = s
            return s

        lax.fori_loop(0, steps - 1, step, s_in, unroll=3)
        re, im = xre[g], xim[g]
        parts = [jnp.where(low, re, swap(im))]
        if wide:
            parts.append(jnp.where(low, swap(re), im))
        for h, x in enumerate(parts):
            smv[g, :, h * LANES:(h + 1) * LANES] = x
            shv[g, :, h * LANES:(h + 1) * LANES] = x.astype(jnp.bfloat16)

    def ag_copy(g, s):
        return pltpu.make_async_remote_copy(
            src_ref=shv.at[g], dst_ref=sh_hbm.at[mp, g],
            send_sem=ag_send.at[g, s - 1], recv_sem=ag_recv.at[g, s - 1],
            device_id=(me, panel(s)), device_id_type=MESH,
        )

    def out_copies(g):
        return (
            pltpu.make_async_copy(shv.at[g], sh_hbm.at[mp, g], out_sem.at[g, 0]),
            pltpu.make_async_copy(smv.at[g], sm_hbm.at[g], out_sem.at[g, 1]),
        )

    for g in range(groups):
        gather_info(g)
        local_map(g)
        each_peer(lambda s: cm_copy(g, s).start())
    for g in range(groups):
        each_peer(lambda s: cm_copy(g, s).wait_recv())
        finish(g)
        for s in range(1, pn):
            ag_copy(g, s).start()
        for copy in out_copies(g):
            copy.start()
    for g in range(groups):
        for s in range(1, pn):
            rs_copy(g, s).wait_send()
        each_peer(lambda s: cm_copy(g, s).wait_send())
        for copy in out_copies(g):
            copy.wait()
        for s in range(1, pn):
            ag_copy(g, s).wait()


def predict_kernel(pn, groups, gw, tile_group, readout, sh, sm, predicted, smoothed):
    total = None
    for p in range(pn):
        for g in range(groups):
            first = (p * groups + g) * gw
            term = lax.dot_general(
                readout[:, first:first + gw], sh[p, g],
                (((1,), (1,)), ((), ())), preferred_element_type=jnp.float32,
            )
            total = term if total is None else total + term
    predicted[...] = total.astype(jnp.bfloat16)
    smoothed[...] = sm[0].T


def body(observations, info_weight, readout, labels, rate, angle, gain):
    units, bins = observations.shape
    n, pn = lax.axis_size("tm"), lax.axis_size("panel")
    lat = info_weight.shape[1] // pn
    gw = 2 * LANES if lat % (2 * LANES) == 0 else LANES
    groups = lat // gw
    regimes = rate.shape[0]
    steps = bins // CHUNKS

    mag = jnp.exp(-rate)
    spread = -jnp.expm1(-2.0 * rate)
    table = jnp.stack([mag * jnp.cos(angle), mag * jnp.sin(angle), gain * jnp.sqrt(spread), spread])
    table = table.reshape(4 * regimes, groups, gw // 2)
    table = jnp.pad(table, ((0, 0), (0, 0), (0, LANES - gw // 2))).reshape(4 * regimes, groups * LANES)
    lab = jnp.broadcast_to(labels.reshape(CHUNKS, steps).T.reshape(bins, 1), (bins, LANES))

    f32, bf16 = jnp.float32, jnp.bfloat16
    vm = pltpu.VMEM
    dma = pltpu.SemaphoreType.DMA
    big = (groups, bins, LANES)
    peers = max(pn - 1, 1)
    sm, sh = pl.pallas_call(
        functools.partial(smooth_kernel, n, pn, groups, gw, regimes),
        out_shape=(
            jax.ShapeDtypeStruct((groups, bins, gw), f32),
            jax.ShapeDtypeStruct((pn, groups, bins, gw), bf16),
        ),
        in_specs=[pl.BlockSpec(memory_space=pl.ANY)] * 2 + [pl.BlockSpec(memory_space=vm)] * 2,
        out_specs=[pl.BlockSpec(memory_space=pl.ANY)] * 2,
        scratch_shapes=[
            vm((units, bins), bf16),
            vm((bins, units), bf16),
            vm((pn, units, lat), bf16),
            vm((bins, lat), f32),
            vm((groups, peers, bins, gw), bf16),
            vm((groups, peers, bins, gw), bf16),
        ] + [vm(big, f32)] * 9 + [
            vm((groups, 13, CHUNKS, LANES), f32),
            vm((groups, n, ROWS, LANES), f32),
            vm((groups, n, 8, LANES), f32),
            vm((groups, 4, CHUNKS, LANES), f32),
            vm((groups, bins, gw), f32),
            vm((groups, bins, gw), bf16),
            dma((pn + 1,)),
            dma((groups, peers)),
            dma((groups, peers)),
            dma((groups, n)),
            dma((groups, n)),
            dma((groups, peers)),
            dma((groups, peers)),
            dma((groups, 2)),
        ],
        compiler_params=pltpu.CompilerParams(
            collective_id=0, has_side_effects=True, vmem_limit_bytes=36 * 2**20
        ),
        cost_estimate=pl.CostEstimate(
            flops=2 * units * bins * lat * pn, bytes_accessed=2 * units * (bins + lat * pn),
            transcendentals=0,
        ),
        name="smooth",
    )(observations, info_weight, lab, table)

    tiles = lat // LANES
    rows = readout.shape[0] // tiles
    per = gw // LANES
    predicted, smoothed = pl.pallas_call(
        functools.partial(predict_kernel, pn, groups, gw, per),
        grid=(tiles,),
        out_shape=(
            jax.ShapeDtypeStruct((readout.shape[0], bins), bf16),
            jax.ShapeDtypeStruct((lat, bins), f32),
        ),
        in_specs=[
            pl.BlockSpec((rows, lat * pn), lambda i: (i, 0)),
            pl.BlockSpec((pn, groups, bins, gw), lambda i: (0, 0, 0, 0)),
            pl.BlockSpec((1, bins, LANES), lambda i: (i // per, 0, i % per)),
        ],
        out_specs=[
            pl.BlockSpec((rows, bins), lambda i: (i, 0)),
            pl.BlockSpec((LANES, bins), lambda i: (i, 0)),
        ],
        compiler_params=pltpu.CompilerParams(vmem_limit_bytes=24 * 2**20),
        cost_estimate=pl.CostEstimate(
            flops=2 * readout.shape[0] * bins * lat * pn,
            bytes_accessed=2 * readout.shape[0] * (lat * pn + bins) + 8 * bins * lat,
            transcendentals=0,
        ),
        name="predict",
    )(readout, sh, sm)
    return (smoothed, predicted)


def solution(mesh):
    return jax.shard_map(
        body,
        mesh=mesh,
        in_specs=(
            P("panel", "tm"),
            P("panel", None),
            P("panel", None),
            P("tm"),
            P(None, "panel"),
            P(None, "panel"),
            P(None, "panel"),
        ),
        out_specs=(P("panel", "tm"), P("panel", "tm")),
        check_vma=False,
    )
```

```python
import functools

import jax
import jax.numpy as jnp
from jax import lax
from jax.experimental import pallas as pl
from jax.experimental.pallas import tpu as pltpu
from jax.sharding import PartitionSpec as P

LANES = 128
HALF = 64
CHUNKS = 8
ROWS = 16
MESH = pl.DeviceIdType.MESH


def mul(x, y):
    return x[0] * y[0] - x[1] * y[1], x[0] * y[1] + x[1] * y[0]


def cmul(x, y):
    return x[0] * y[0] + x[1] * y[1], x[0] * y[1] - x[1] * y[0]


def add(x, y):
    return x[0] + y[0], x[1] + y[1]


def smooth_kernel(
    n, pn, groups, gw, regimes,
    obs_hbm, w_hbm, lab_hbm, rate_hbm, angle_hbm, gain_hbm,
    sm_hbm, sh_hbm,
    obs, obs_t, w, own, rs_out, rs_in, xre, xim, are, aim, scl, vre, vim, coef, mre, mim, pre, pim,
    lab_ref, rate_ref, angle_ref, gain_ref, lab, lab_rows, chunk, msgs, enter, bound, smv, shv,
    in_sem, small_sem, rs_send, rs_recv, cm_send, cm_recv, ag_send, ag_recv, out_sem,
):
    me = lax.axis_index("tm")
    mp = lax.axis_index("panel")
    units, bins = obs.shape
    lat = own.shape[1]
    steps = bins // CHUNKS
    wide = gw == 2 * LANES

    def panel(s):
        return lax.rem(mp + s, pn)

    obs_copy = pltpu.make_async_copy(obs_hbm, obs, in_sem.at[0])
    obs_copy.start()
    w_copies = {}
    for s in list(range(1, pn)) + [0]:
        columns = pl.ds(pl.multiple_of(panel(s) * lat, LANES), lat)
        w_copies[s] = pltpu.make_async_copy(w_hbm.at[:, columns], w.at[s], in_sem.at[1 + s])
        w_copies[s].start()

    small_copies = [
        pltpu.make_async_copy(src, dst, small_sem.at[i])
        for i, (src, dst) in enumerate((
            (lab_hbm, lab_ref), (rate_hbm, rate_ref), (angle_hbm, angle_ref), (gain_hbm, gain_ref)
        ))
    ]
    for copy in small_copies:
        copy.start()

    barrier = pltpu.get_barrier_semaphore()

    for s in range(1, pn):
        pl.semaphore_signal(barrier, inc=1, device_id=(me, panel(s)), device_id_type=MESH)

    def greet(s, _):
        pl.semaphore_signal(
            barrier, inc=1, device_id=(lax.rem(me + s, n), mp), device_id_type=MESH
        )
        return 0

    lax.fori_loop(1, n, greet, 0)

    def rows_of(k):
        return pl.ds(pl.multiple_of(k * CHUNKS, CHUNKS), CHUNKS)

    def spread_labels():
        for c in range(CHUNKS):
            row, first = divmod(c * steps, LANES)
            x = lab_ref[row:row + 1, :]
            lab_rows[c:c + 1, :] = x if first == 0 else pltpu.roll(x, LANES - first, 1)
        x = lab_rows[...]
        for k in range(steps):
            lab[k * CHUNKS:(k + 1) * CHUNKS, :] = jnp.broadcast_to(x[:, k:k + 1], (CHUNKS, LANES))

    def prepare(g):
        lanes = slice(g * LANES, (g + 1) * LANES)
        rate, angle = rate_ref[:, lanes], angle_ref[:, lanes]
        x = 2.0 * rate
        series = 1.0 - x * (1.0 / 8.0)
        for term in range(7, 1, -1):
            series = 1.0 - x * (1.0 / term) * series
        spread = jnp.where(x < 0.25, x * series, 1.0 - jnp.exp(-x))
        mag = jnp.exp(-rate)
        values = (
            mag * jnp.cos(angle), mag * jnp.sin(angle),
            gain_ref[:, lanes] * jnp.sqrt(spread), spread,
        )
        table = [
            [jnp.broadcast_to(v[r:r + 1, :], (CHUNKS, LANES)) for r in range(regimes)]
            for v in values
        ]

        def at(k):
            label = lab[rows_of(k), :]
            which = [label == r for r in range(regimes)]

            def pick(q):
                value = table[q][0]
                for r in range(1, regimes):
                    value = jnp.where(which[r], table[q][r], value)
                return value

            return (pick(0), pick(1)), pick(2), pick(3)

        def keep(k, a, scale, c, p):
            rows = rows_of(k)
            are[g, rows, :], aim[g, rows, :] = a
            scl[g, rows, :], coef[g, rows, :] = scale, c
            pre[g, rows, :], pim[g, rows, :] = p

        def step(k, carry):
            p, q, d = carry
            a, scale, c = at(k)
            v = (c * q[0], -(c * q[1]))
            before = rows_of(k - 1)
            vre[g, before, :], vim[g, before, :] = v
            d = add(d, mul(v, p))
            p, q = mul(a, p), mul(a, q)
            keep(k, a, scale, c, p)
            return p, q, d

        zero = jnp.zeros((CHUNKS, LANES), jnp.float32)
        one = jnp.ones((CHUNKS, LANES), jnp.float32)
        a0, scale0, c0 = at(0)
        keep(0, a0, scale0, c0, a0)
        p, q, d = lax.fori_loop(1, steps, step, (a0, (one, zero), (zero, zero)), unroll=3)
        end = rows_of(steps - 1)
        vre[g, end, :], vim[g, end, :] = zero, zero
        for row, x in zip((0, 1, 4, 5, 8, 9, 10, 11, 12), (*p, q[0], -q[1], *d, *a0, c0)):
            chunk[g, row] = x

    obs_copy.wait()
    tile = 256

    def turn(i, _):
        rows = pl.ds(pl.multiple_of(i * tile, tile), tile)
        obs_t[:, rows] = obs[rows, :].T
        return 0

    lax.fori_loop(0, units // tile, turn, 0)

    def rs_copy(g, s):
        return pltpu.make_async_remote_copy(
            src_ref=rs_out.at[g, s - 1], dst_ref=rs_in.at[g, s - 1],
            send_sem=rs_send.at[g, s - 1], recv_sem=rs_recv.at[g, s - 1],
            device_id=(me, panel(s)), device_id_type=MESH,
        )

    def project(g, s):
        return jnp.dot(
            obs_t[...], w[s, :, g * gw:(g + 1) * gw], preferred_element_type=jnp.float32
        )

    for s in range(1, pn):
        w_copies[s].wait()
    for g in range(groups):
        for s in range(1, pn):
            rs_out[g, s - 1] = project(g, s).astype(jnp.bfloat16)
            if g == 0 and s == 1:
                pl.semaphore_wait(barrier, n - 1 + pn - 1)
            rs_copy(g, s).start()
    w_copies[0].wait()
    for g in range(groups):
        own[:, g * gw:(g + 1) * gw] = project(g, 0)

    for copy in small_copies:
        copy.wait()
    spread_labels()
    for g in range(groups):
        prepare(g)

    lane = lax.broadcasted_iota(jnp.int32, (bins, LANES), 1)
    low = lane < HALF

    def swap(x):
        return pltpu.roll(x, HALF, 1)

    def gather_info(g):
        for s in range(1, pn):
            rs_copy(g, s).wait_recv()
        parts = []
        for h in range(gw // LANES):
            x = own[:, g * gw + h * LANES:g * gw + (h + 1) * LANES]
            for s in range(1, pn):
                x = x + rs_in[g, s - 1, :, h * LANES:(h + 1) * LANES].astype(jnp.float32)
            parts.append(x)
        if wide:
            xre[g] = jnp.where(low, parts[0], swap(parts[1]))
            xim[g] = jnp.where(low, swap(parts[0]), parts[1])
        else:
            xre[g] = parts[0]
            xim[g] = swap(parts[0])

    def scan(g):
        def step(k, carry):
            m, e = carry
            rows = rows_of(k)
            bin_rows = pl.ds(k, CHUNKS, stride=steps)
            scale = scl[g, rows, :]
            u = (scale * xre[g, bin_rows, :], scale * xim[g, bin_rows, :])
            m = add(mul((are[g, rows, :], aim[g, rows, :]), m), u)
            e = add(e, mul((vre[g, rows, :], vim[g, rows, :]), m))
            mre[g, rows, :], mim[g, rows, :] = m
            return m, e

        zero = jnp.zeros((CHUNKS, LANES), jnp.float32)
        b, e = lax.fori_loop(0, steps, step, ((zero, zero), (zero, zero)), unroll=4)
        chunk[g, 2], chunk[g, 3] = b
        chunk[g, 6], chunk[g, 7] = e

    def chunk_row(g, q, c):
        return chunk[g, q, c:c + 1, :]

    def chunk_map(g, c):
        v = [chunk_row(g, q, c) for q in range(13)]
        return (v[0], v[1]), (v[2], v[3]), (v[4], v[5]), (v[6], v[7]), (v[8], v[9]), (v[10], v[11]), v[12]

    def local_map(g):
        scan(g)
        A, B, G, E, D, a0, c0 = chunk_map(g, 0)
        for c in range(1, CHUNKS):
            Ar, Br, Gr, Er, Dr, ar, cr = chunk_map(g, c)
            K = cmul(ar, Dr)
            K = (K[0] + cr, K[1])
            E = add(E, mul(G, add(cmul(ar, Er), mul(K, B))))
            D = add(D, mul(G, mul(K, A)))
            G = mul(G, cmul(ar, Gr))
            A, B = mul(Ar, A), add(mul(Ar, B), Br)
        rows = (*A, *B, *G, *E, *D, *a0, c0)
        for q in range(13):
            msgs[g, 0, q:q + 1, :] = rows[q]
        msgs[g, 0, 13:ROWS, :] = jnp.zeros((ROWS - 13, LANES), jnp.float32)

    def cm_copy(g, s):
        return pltpu.make_async_remote_copy(
            src_ref=msgs.at[g, 0], dst_ref=msgs.at[g, s],
            send_sem=cm_send.at[g, s], recv_sem=cm_recv.at[g, s],
            device_id=(lax.rem(me + s, n), mp), device_id_type=MESH,
        )

    def each_peer(act):
        def go(s, _):
            act(s)
            return 0

        lax.fori_loop(1, n, go, 0)

    def boundary(g):
        zero = jnp.zeros((1, LANES), jnp.float32)

        def pair(slot, q):
            return msgs[g, slot, q:q + 1, :], msgs[g, slot, q + 1:q + 2, :]

        def put(d, row, value):
            enter[g, d, row:row + 1, :], enter[g, d, row + 1:row + 2, :] = value

        def get(d, row):
            return enter[g, d, row:row + 1, :], enter[g, d, row + 1:row + 2, :]

        def ahead(d, m):
            slot = lax.rem(me - d + n, n)
            put(d, 0, m)
            return add(mul(pair(slot, 0), m), pair(slot, 2))

        last = lax.fori_loop(0, n, ahead, (zero, zero), unroll=4)

        def back(i, s):
            d = n - 1 - i
            slot = lax.rem(me - d + n, n)
            put(d, 2, s)
            m = get(d, 0)
            first = add(add(mul(pair(slot, 4), s), pair(slot, 6)), mul(pair(slot, 8), m))
            c = msgs[g, slot, 12:13, :]
            return add(cmul(pair(slot, 10), first), (c * m[0], c * m[1]))

        lax.fori_loop(0, n, back, last, unroll=4)
        m_in, s_in = get(me, 0), get(me, 2)
        return m_in, s_in

    def finish(g):
        m, s = boundary(g)
        entering = []
        for c in range(CHUNKS):
            entering.append(m)
            bound[g, 0, c:c + 1, :], bound[g, 1, c:c + 1, :] = m
            A, B = chunk_map(g, c)[:2]
            m = add(mul(A, m), B)
        for c in reversed(range(CHUNKS)):
            bound[g, 2, c:c + 1, :], bound[g, 3, c:c + 1, :] = s
            _, _, G, E, D, a0, c0 = chunk_map(g, c)
            m = entering[c]
            first = add(add(mul(G, s), E), mul(D, m))
            s = add(cmul(a0, first), (c0 * m[0], c0 * m[1]))
        m_in = (bound[g, 0], bound[g, 1])
        s_in = (bound[g, 2], bound[g, 3])
        end = pl.ds(steps - 1, CHUNKS, stride=steps)
        xre[g, end, :], xim[g, end, :] = s_in

        def step(i, s):
            k = steps - 2 - i
            rows, after = rows_of(k), rows_of(k + 1)
            a = (are[g, after, :], aim[g, after, :])
            c = coef[g, after, :]
            m = add((mre[g, rows, :], mim[g, rows, :]), mul((pre[g, rows, :], pim[g, rows, :]), m_in))
            s = add(cmul(a, s), (c * m[0], c * m[1]))
            bin_rows = pl.ds(k, CHUNKS, stride=steps)
            xre[g, bin_rows, :], xim[g, bin_rows, :] = s
            return s

        lax.fori_loop(0, steps - 1, step, s_in, unroll=3)
        re, im = xre[g], xim[g]
        parts = [jnp.where(low, re, swap(im))]
        if wide:
            parts.append(jnp.where(low, swap(re), im))
        for h, x in enumerate(parts):
            smv[g, :, h * LANES:(h + 1) * LANES] = x
            shv[g, :, h * LANES:(h + 1) * LANES] = x.astype(jnp.bfloat16)

    def sh_columns(g):
        return pl.ds(pl.multiple_of(mp * lat + g * gw, LANES), gw)

    def ag_copy(g, s):
        return pltpu.make_async_remote_copy(
            src_ref=shv.at[g], dst_ref=sh_hbm.at[:, sh_columns(g)],
            send_sem=ag_send.at[g, s - 1], recv_sem=ag_recv.at[g, s - 1],
            device_id=(me, panel(s)), device_id_type=MESH,
        )

    def out_copies(g):
        return (
            pltpu.make_async_copy(shv.at[g], sh_hbm.at[:, sh_columns(g)], out_sem.at[g, 0]),
            pltpu.make_async_copy(smv.at[g], sm_hbm.at[g], out_sem.at[g, 1]),
        )

    for g in range(groups):
        gather_info(g)
        local_map(g)
        each_peer(lambda s: cm_copy(g, s).start())
        each_peer(lambda s: cm_copy(g, s).wait_recv())
        finish(g)
        for s in range(1, pn):
            ag_copy(g, s).start()
        for copy in out_copies(g):
            copy.start()
    for g in range(groups):
        for s in range(1, pn):
            rs_copy(g, s).wait_send()
        each_peer(lambda s: cm_copy(g, s).wait_send())
        for copy in out_copies(g):
            copy.wait()
        for s in range(1, pn):
            ag_copy(g, s).wait()


def predict_kernel(
    tiles, readout_hbm, sh_hbm, sm_hbm, predicted, smoothed,
    readout, sh, sm, out, turned, in_sems, sems,
):
    rows = readout.shape[0] // tiles
    per = sm.shape[2] // LANES
    loads, copies = [], []

    def send(src, dst):
        copy = pltpu.make_async_copy(src, dst, sems.at[len(copies)])
        copy.start()
        copies.append(copy)

    def fetch(src, dst):
        load = pltpu.make_async_copy(src, dst, in_sems.at[len(loads)])
        load.start()
        loads.append(load)

    fetch(sh_hbm, sh)
    for i in range(tiles):
        part = pl.ds(i * rows, rows)
        fetch(readout_hbm.at[part], readout.at[part])
        if i == 0:
            fetch(sm_hbm, sm)
    sh_load, first, sm_load, *later = loads
    loads = [first, *later]
    sh_load.wait()
    for i in range(tiles):
        lanes = slice(i * LANES, (i + 1) * LANES)
        here = slice((i % per) * LANES, (i % per + 1) * LANES)
        part = pl.ds(i * rows, rows)
        loads[i].wait()
        out[part, :] = lax.dot_general(
            readout[part, :], sh[...],
            (((1,), (1,)), ((), ())), preferred_element_type=jnp.float32,
        ).astype(jnp.bfloat16)
        send(out.at[part], predicted.at[part])
        if i == 0:
            sm_load.wait()
        turned[lanes, :] = sm[i // per, :, here].T
        send(turned.at[pl.ds(i * LANES, LANES)], smoothed.at[pl.ds(i * LANES, LANES)])
    for copy in copies:
        copy.wait()


def body(observations, info_weight, readout, labels, rate, angle, gain):
    units, bins = observations.shape
    n, pn = lax.axis_size("tm"), lax.axis_size("panel")
    lat = info_weight.shape[1] // pn
    gw = 2 * LANES if lat % (2 * LANES) == 0 else LANES
    groups = lat // gw
    regimes = rate.shape[0]

    short = groups * LANES - rate.shape[1]
    if short:
        rate, angle, gain = (
            jnp.pad(x, ((0, 0), (0, short)), constant_values=0.25) for x in (rate, angle, gain)
        )
    lab = labels.reshape(bins // LANES, LANES)

    f32, bf16 = jnp.float32, jnp.bfloat16
    vm = pltpu.VMEM
    dma = pltpu.SemaphoreType.DMA
    big = (groups, bins, LANES)
    peers = max(pn - 1, 1)
    sm, sh = pl.pallas_call(
        functools.partial(smooth_kernel, n, pn, groups, gw, regimes),
        out_shape=(
            jax.ShapeDtypeStruct((groups, bins, gw), f32),
            jax.ShapeDtypeStruct((bins, pn * lat), bf16),
        ),
        in_specs=[pl.BlockSpec(memory_space=pl.ANY)] * 6,
        out_specs=[pl.BlockSpec(memory_space=pl.ANY)] * 2,
        scratch_shapes=[
            vm((units, bins), bf16),
            vm((bins, units), bf16),
            vm((pn, units, lat), bf16),
            vm((bins, lat), f32),
            vm((groups, peers, bins, gw), bf16),
            vm((groups, peers, bins, gw), bf16),
        ] + [vm(big, f32)] * 12 + [
            vm((bins // LANES, LANES), jnp.int32),
        ] + [vm(rate.shape, f32)] * 3 + [
            vm((bins, LANES), jnp.int32),
            vm((CHUNKS, LANES), jnp.int32),
            vm((groups, 13, CHUNKS, LANES), f32),
            vm((groups, n, ROWS, LANES), f32),
            vm((groups, n, 8, LANES), f32),
            vm((groups, 4, CHUNKS, LANES), f32),
            vm((groups, bins, gw), f32),
            vm((groups, bins, gw), bf16),
            dma((pn + 1,)),
            dma((4,)),
            dma((groups, peers)),
            dma((groups, peers)),
            dma((groups, n)),
            dma((groups, n)),
            dma((groups, peers)),
            dma((groups, peers)),
            dma((groups, 2)),
        ],
        compiler_params=pltpu.CompilerParams(
            collective_id=0, has_side_effects=True, vmem_limit_bytes=61 * 2**20
        ),
        cost_estimate=pl.CostEstimate(
            flops=2 * units * bins * lat * pn, bytes_accessed=2 * units * (bins + lat * pn),
            transcendentals=0,
        ),
        name="smooth",
    )(observations, info_weight, lab, rate, angle, gain)

    tiles = lat // LANES
    predicted, smoothed = pl.pallas_call(
        functools.partial(predict_kernel, tiles),
        out_shape=(
            jax.ShapeDtypeStruct((readout.shape[0], bins), bf16),
            jax.ShapeDtypeStruct((lat, bins), f32),
        ),
        in_specs=[pl.BlockSpec(memory_space=pl.ANY)] * 3,
        out_specs=[pl.BlockSpec(memory_space=pltpu.HBM)] * 2,
        scratch_shapes=[
            vm(readout.shape, bf16),
            vm(sh.shape, bf16),
            vm(sm.shape, f32),
            vm((readout.shape[0], bins), bf16),
            vm((lat, bins), f32),
            dma((tiles + 2,)),
            dma((2 * tiles,)),
        ],
        compiler_params=pltpu.CompilerParams(vmem_limit_bytes=61 * 2**20),
        cost_estimate=pl.CostEstimate(
            flops=2 * readout.shape[0] * bins * lat * pn,
            bytes_accessed=2 * readout.shape[0] * (lat * pn + bins) + 8 * bins * lat,
            transcendentals=0,
        ),
        name="predict",
    )(readout, sh, sm)
    return (smoothed, predicted)


def solution(mesh):
    return jax.shard_map(
        body,
        mesh=mesh,
        in_specs=(
            P("panel", "tm"),
            P("panel", None),
            P("panel", None),
            P("tm"),
            P(None, "panel"),
            P(None, "panel"),
            P(None, "panel"),
        ),
        out_specs=(P("panel", "tm"), P("panel", "tm")),
        check_vma=False,
    )
```

```python
import functools

import jax
import jax.numpy as jnp
from jax import lax
from jax.experimental import pallas as pl
from jax.experimental.pallas import tpu as pltpu
from jax.sharding import PartitionSpec as P

LANES = 128
HALF = 64
CHUNKS = 8
TURN = 256
FIXED = 9
MESH = pl.DeviceIdType.MESH


def mul(x, y):
    return x[0] * y[0] - x[1] * y[1], x[0] * y[1] + x[1] * y[0]


def cmul(x, y):
    return x[0] * y[0] + x[1] * y[1], x[0] * y[1] - x[1] * y[0]


def add(x, y):
    return x[0] + y[0], x[1] + y[1]


def smooth_kernel(
    n, pn, groups, gw, regimes,
    obs_hbm, w_hbm, lab_hbm, rate_hbm, angle_hbm, gain_hbm,
    sm_hbm, sh_hbm,
    obs, obs_t, w, own, rs_out, rs_in, xre, xim, are, aim, scl, vre, vim, coef, mre, mim, pre, pim,
    lab_ref, rate_ref, angle_ref, gain_ref, lab, lab_rows, chunk, joint, fixed, moving, enter, bound, smv, smt, shv,
    obs_sem, w_sem, small_sem, rs_send, rs_recv, fx_send, fx_recv, cm_send, cm_recv, ag_send, ag_recv, out_sem,
):
    me = lax.axis_index("tm")
    mp = lax.axis_index("panel")
    units, bins = obs.shape
    lat = own.shape[1]
    steps = bins // CHUNKS
    wide = gw == 2 * LANES

    def panel(s):
        return lax.rem(mp + s, pn)

    turns = units // TURN

    def obs_copy(i):
        rows = pl.ds(pl.multiple_of(i * TURN, TURN), TURN)
        return pltpu.make_async_copy(obs_hbm.at[rows], obs.at[rows], obs_sem.at[i])

    def w_copy(g, s):
        columns = pl.ds(pl.multiple_of(panel(s) * lat + g * gw, LANES), gw)
        return pltpu.make_async_copy(w_hbm.at[:, columns], w.at[s, g], w_sem.at[s, g])

    def load(i, _):
        obs_copy(i).start()
        return 0

    lax.fori_loop(0, turns, load, 0)
    for g in range(groups):
        for s in range(1, pn):
            w_copy(g, s).start()
    for g in range(groups):
        w_copy(g, 0).start()

    small_copies = [
        pltpu.make_async_copy(src, dst, small_sem.at[i])
        for i, (src, dst) in enumerate((
            (lab_hbm, lab_ref), (rate_hbm, rate_ref), (angle_hbm, angle_ref), (gain_hbm, gain_ref)
        ))
    ]
    for copy in small_copies:
        copy.start()

    barrier = pltpu.get_barrier_semaphore()

    for s in range(1, pn):
        pl.semaphore_signal(barrier, inc=1, device_id=(me, panel(s)), device_id_type=MESH)

    def greet(s, _):
        pl.semaphore_signal(
            barrier, inc=1, device_id=(lax.rem(me + s, n), mp), device_id_type=MESH
        )
        return 0

    lax.fori_loop(1, n, greet, 0)

    def rows_of(k):
        return pl.ds(pl.multiple_of(k * CHUNKS, CHUNKS), CHUNKS)

    def spread_labels():
        for c in range(CHUNKS):
            row, first = divmod(c * steps, LANES)
            x = lab_ref[row:row + 1, :]
            lab_rows[c:c + 1, :] = x if first == 0 else pltpu.roll(x, LANES - first, 1)
        x = lab_rows[...]
        for k in range(steps):
            lab[k * CHUNKS:(k + 1) * CHUNKS, :] = jnp.broadcast_to(x[:, k:k + 1], (CHUNKS, LANES))

    def prepare(g):
        lanes = slice(g * LANES, (g + 1) * LANES)
        rate, angle = rate_ref[:, lanes], angle_ref[:, lanes]
        x = 2.0 * rate
        series = 1.0 - x * (1.0 / 8.0)
        for term in range(7, 1, -1):
            series = 1.0 - x * (1.0 / term) * series
        spread = jnp.where(x < 0.25, x * series, 1.0 - jnp.exp(-x))
        mag = jnp.exp(-rate)
        values = (
            mag * jnp.cos(angle), mag * jnp.sin(angle),
            gain_ref[:, lanes] * jnp.sqrt(spread), spread,
        )
        table = [
            [jnp.broadcast_to(v[r:r + 1, :], (CHUNKS, LANES)) for r in range(regimes)]
            for v in values
        ]

        def at(k):
            label = lab[rows_of(k), :]
            which = [label == r for r in range(regimes)]

            def pick(q):
                value = table[q][0]
                for r in range(1, regimes):
                    value = jnp.where(which[r], table[q][r], value)
                return value

            return (pick(0), pick(1)), pick(2), pick(3)

        def keep(k, a, scale, c, p):
            rows = rows_of(k)
            are[g, rows, :], aim[g, rows, :] = a
            scl[g, rows, :], coef[g, rows, :] = scale, c
            pre[g, rows, :], pim[g, rows, :] = p

        def step(k, carry):
            p, q, d = carry
            a, scale, c = at(k)
            v = (c * q[0], -(c * q[1]))
            before = rows_of(k - 1)
            vre[g, before, :], vim[g, before, :] = v
            d = add(d, mul(v, p))
            p, q = mul(a, p), mul(a, q)
            keep(k, a, scale, c, p)
            return p, q, d

        zero = jnp.zeros((CHUNKS, LANES), jnp.float32)
        one = jnp.ones((CHUNKS, LANES), jnp.float32)
        a0, scale0, c0 = at(0)
        keep(0, a0, scale0, c0, a0)
        p, q, d = lax.fori_loop(1, steps, step, (a0, (one, zero), (zero, zero)), unroll=3)
        end = rows_of(steps - 1)
        vre[g, end, :], vim[g, end, :] = zero, zero
        for row, x in zip((0, 1, 4, 5, 8, 9, 10, 11, 12), (*p, q[0], -q[1], *d, *a0, c0)):
            chunk[g, row] = x

    def chunk_row(g, q, c):
        return chunk[g, q, c:c + 1, :]

    def pair_row(g, q, c):
        return chunk_row(g, q, c), chunk_row(g, q + 1, c)

    def chunk_map(g, c):
        return *(pair_row(g, q, c) for q in (0, 4, 8, 10)), chunk_row(g, 12, c)

    def join_fixed(g):
        A, G, D, a0, c0 = chunk_map(g, 0)
        for c in range(1, CHUNKS):
            Ar, Gr, Dr, ar, cr = chunk_map(g, c)
            K = cmul(ar, Dr)
            K = mul(G, (K[0] + cr, K[1]))
            M = mul(G, (ar[0], -ar[1]))
            for row, x in enumerate((*M, *K)):
                joint[g, row, c:c + 1, :] = x
            D = add(D, mul(K, A))
            G = mul(M, Gr)
            A = mul(Ar, A)
        for row, x in enumerate((*A, *G, *D, *a0, c0)):
            fixed[0, g * FIXED + row:g * FIXED + row + 1, :] = x
        last = groups * FIXED
        if g == groups - 1 and last < fixed.shape[1]:
            fixed[0, last:, :] = jnp.zeros((fixed.shape[1] - last, LANES), jnp.float32)

    def turn(i, _):
        obs_copy(i).wait()
        rows = pl.ds(pl.multiple_of(i * TURN, TURN), TURN)
        obs_t[:, rows] = obs[rows, :].T
        return 0

    lax.fori_loop(0, turns, turn, 0)

    def rs_copy(g, s):
        return pltpu.make_async_remote_copy(
            src_ref=rs_out.at[g, s - 1], dst_ref=rs_in.at[g, s - 1],
            send_sem=rs_send.at[g, s - 1], recv_sem=rs_recv.at[g, s - 1],
            device_id=(me, panel(s)), device_id_type=MESH,
        )

    def project(g, s):
        w_copy(g, s).wait()
        return jnp.dot(obs_t[...], w[s, g], preferred_element_type=jnp.float32)

    for g in range(groups):
        for s in range(1, pn):
            rs_out[g, s - 1] = project(g, s).astype(jnp.bfloat16)
            if g == 0 and s == 1:
                pl.semaphore_wait(barrier, n - 1 + pn - 1)
            rs_copy(g, s).start()

    def each_peer(act):
        def go(s, _):
            act(s)
            return 0

        lax.fori_loop(1, n, go, 0)

    def fx_copy(s):
        return pltpu.make_async_remote_copy(
            src_ref=fixed.at[0], dst_ref=fixed.at[s],
            send_sem=fx_send.at[s], recv_sem=fx_recv.at[s],
            device_id=(lax.rem(me + s, n), mp), device_id_type=MESH,
        )

    for copy in small_copies:
        copy.wait()
    spread_labels()
    for g in range(groups):
        prepare(g)
        join_fixed(g)
    each_peer(lambda s: fx_copy(s).start())
    for g in range(groups):
        own[:, g * gw:(g + 1) * gw] = project(g, 0)

    lane = lax.broadcasted_iota(jnp.int32, (bins, LANES), 1)
    low = lane < HALF

    def swap(x):
        return pltpu.roll(x, HALF, 1)

    def gather_info(g):
        for s in range(1, pn):
            rs_copy(g, s).wait_recv()
        parts = []
        for h in range(gw // LANES):
            x = own[:, g * gw + h * LANES:g * gw + (h + 1) * LANES]
            for s in range(1, pn):
                x = x + rs_in[g, s - 1, :, h * LANES:(h + 1) * LANES].astype(jnp.float32)
            parts.append(x)
        if wide:
            xre[g] = jnp.where(low, parts[0], swap(parts[1]))
            xim[g] = jnp.where(low, swap(parts[0]), parts[1])
        else:
            xre[g] = parts[0]
            xim[g] = swap(parts[0])

    def scan(g):
        def step(k, carry):
            m, e = carry
            rows = rows_of(k)
            bin_rows = pl.ds(k, CHUNKS, stride=steps)
            scale = scl[g, rows, :]
            u = (scale * xre[g, bin_rows, :], scale * xim[g, bin_rows, :])
            m = add(mul((are[g, rows, :], aim[g, rows, :]), m), u)
            e = add(e, mul((vre[g, rows, :], vim[g, rows, :]), m))
            mre[g, rows, :], mim[g, rows, :] = m
            return m, e

        zero = jnp.zeros((CHUNKS, LANES), jnp.float32)
        b, e = lax.fori_loop(0, steps, step, ((zero, zero), (zero, zero)), unroll=4)
        chunk[g, 2], chunk[g, 3] = b
        chunk[g, 6], chunk[g, 7] = e

    def local_map(g):
        scan(g)
        B, E = pair_row(g, 2, 0), pair_row(g, 6, 0)
        for c in range(1, CHUNKS):
            M = (joint[g, 0, c:c + 1, :], joint[g, 1, c:c + 1, :])
            K = (joint[g, 2, c:c + 1, :], joint[g, 3, c:c + 1, :])
            E = add(E, add(mul(M, pair_row(g, 6, c)), mul(K, B)))
            B = add(mul(pair_row(g, 0, c), B), pair_row(g, 2, c))
        for row, x in enumerate((*B, *E)):
            moving[g, 0, row:row + 1, :] = x

    def cm_copy(g, s):
        return pltpu.make_async_remote_copy(
            src_ref=moving.at[g, 0], dst_ref=moving.at[g, s],
            send_sem=cm_send.at[g, s], recv_sem=cm_recv.at[g, s],
            device_id=(lax.rem(me + s, n), mp), device_id_type=MESH,
        )

    def boundary(g):
        zero = jnp.zeros((1, LANES), jnp.float32)

        def still(slot, q):
            q = g * FIXED + q
            return fixed[slot, q:q + 1, :], fixed[slot, q + 1:q + 2, :]

        def fresh(slot, q):
            return moving[g, slot, q:q + 1, :], moving[g, slot, q + 1:q + 2, :]

        def put(d, row, value):
            enter[g, d, row:row + 1, :], enter[g, d, row + 1:row + 2, :] = value

        def get(d, row):
            return enter[g, d, row:row + 1, :], enter[g, d, row + 1:row + 2, :]

        def ahead(d, m):
            slot = lax.rem(me - d + n, n)
            put(d, 0, m)
            return add(mul(still(slot, 0), m), fresh(slot, 0))

        last = lax.fori_loop(0, n, ahead, (zero, zero), unroll=4)

        def back(i, s):
            d = n - 1 - i
            slot = lax.rem(me - d + n, n)
            put(d, 2, s)
            m = get(d, 0)
            first = add(add(mul(still(slot, 2), s), fresh(slot, 2)), mul(still(slot, 4), m))
            c = fixed[slot, g * FIXED + 8:g * FIXED + 9, :]
            return add(cmul(still(slot, 6), first), (c * m[0], c * m[1]))

        lax.fori_loop(0, n, back, last, unroll=4)
        m_in, s_in = get(me, 0), get(me, 2)
        return m_in, s_in

    def finish(g):
        m, s = boundary(g)
        entering = []
        for c in range(CHUNKS):
            entering.append(m)
            bound[g, 0, c:c + 1, :], bound[g, 1, c:c + 1, :] = m
            m = add(mul(pair_row(g, 0, c), m), pair_row(g, 2, c))
        for c in reversed(range(CHUNKS)):
            bound[g, 2, c:c + 1, :], bound[g, 3, c:c + 1, :] = s
            _, G, D, a0, c0 = chunk_map(g, c)
            m = entering[c]
            first = add(add(mul(G, s), pair_row(g, 6, c)), mul(D, m))
            s = add(cmul(a0, first), (c0 * m[0], c0 * m[1]))
        m_in = (bound[g, 0], bound[g, 1])
        s_in = (bound[g, 2], bound[g, 3])
        end = pl.ds(steps - 1, CHUNKS, stride=steps)
        xre[g, end, :], xim[g, end, :] = s_in

        def step(i, s):
            k = steps - 2 - i
            rows, after = rows_of(k), rows_of(k + 1)
            a = (are[g, after, :], aim[g, after, :])
            c = coef[g, after, :]
            m = add((mre[g, rows, :], mim[g, rows, :]), mul((pre[g, rows, :], pim[g, rows, :]), m_in))
            s = add(cmul(a, s), (c * m[0], c * m[1]))
            bin_rows = pl.ds(k, CHUNKS, stride=steps)
            xre[g, bin_rows, :], xim[g, bin_rows, :] = s
            return s

        lax.fori_loop(0, steps - 1, step, s_in, unroll=3)
        re, im = xre[g], xim[g]
        parts = [jnp.where(low, re, swap(im))]
        if wide:
            parts.append(jnp.where(low, swap(re), im))
        for h, x in enumerate(parts):
            smv[g, :, h * LANES:(h + 1) * LANES] = x
            shv[g, :, h * LANES:(h + 1) * LANES] = x.astype(jnp.bfloat16)

    def sh_columns(g):
        return pl.ds(pl.multiple_of(mp * lat + g * gw, LANES), gw)

    def ag_copy(g, s):
        return pltpu.make_async_remote_copy(
            src_ref=shv.at[g], dst_ref=sh_hbm.at[:, sh_columns(g)],
            send_sem=ag_send.at[g, s - 1], recv_sem=ag_recv.at[g, s - 1],
            device_id=(me, panel(s)), device_id_type=MESH,
        )

    def out_copies(g):
        return (
            pltpu.make_async_copy(shv.at[g], sh_hbm.at[:, sh_columns(g)], out_sem.at[g, 0]),
            pltpu.make_async_copy(smt.at[g], sm_hbm.at[pl.ds(g * gw, gw)], out_sem.at[g, 1]),
        )

    def turn_out(g):
        for h in range(gw // LANES):
            lanes = slice(h * LANES, (h + 1) * LANES)
            smt[g, lanes, :] = smv[g, :, lanes].T
        out_copies(g)[1].start()

    for g in range(groups):
        gather_info(g)
        local_map(g)
        each_peer(lambda s: cm_copy(g, s).start())
        if g == 0:
            each_peer(lambda s: fx_copy(s).wait_recv())
        else:
            turn_out(g - 1)
        each_peer(lambda s: cm_copy(g, s).wait_recv())
        finish(g)
        for s in range(1, pn):
            ag_copy(g, s).start()
        out_copies(g)[0].start()
    turn_out(groups - 1)
    each_peer(lambda s: fx_copy(s).wait_send())
    for g in range(groups):
        for s in range(1, pn):
            rs_copy(g, s).wait_send()
        each_peer(lambda s: cm_copy(g, s).wait_send())
        for copy in out_copies(g):
            copy.wait()
        for s in range(1, pn):
            ag_copy(g, s).wait()


def predict_kernel(
    tiles, readout_hbm, sh_hbm, sm_hbm, predicted, smoothed, readout, sh, out, in_sems, sems
):
    rows = readout.shape[0] // tiles
    loads, copies = [], []

    def begin(into, src, dst, sem):
        into.append(pltpu.make_async_copy(src, dst, sem))
        into[-1].start()

    begin(loads, sh_hbm, sh, in_sems.at[tiles])
    for i in range(tiles):
        part = pl.ds(i * rows, rows)
        begin(loads, readout_hbm.at[part], readout.at[part], in_sems.at[i])
    begin(copies, sm_hbm, smoothed, sems.at[tiles])
    loads[0].wait()
    for i in range(tiles):
        part = pl.ds(i * rows, rows)
        loads[i + 1].wait()
        out[part, :] = lax.dot_general(
            readout[part, :], sh[...],
            (((1,), (1,)), ((), ())), preferred_element_type=jnp.float32,
        ).astype(jnp.bfloat16)
        begin(copies, out.at[part], predicted.at[part], sems.at[i])
    for copy in copies:
        copy.wait()


def body(observations, info_weight, readout, labels, rate, angle, gain):
    units, bins = observations.shape
    n, pn = lax.axis_size("tm"), lax.axis_size("panel")
    lat = info_weight.shape[1] // pn
    gw = 2 * LANES if lat % (2 * LANES) == 0 else LANES
    groups = lat // gw
    regimes = rate.shape[0]

    short = groups * LANES - rate.shape[1]
    if short:
        rate, angle, gain = (
            jnp.pad(x, ((0, 0), (0, short)), constant_values=0.25) for x in (rate, angle, gain)
        )
    lab = labels.reshape(bins // LANES, LANES)

    f32, bf16 = jnp.float32, jnp.bfloat16
    vm = pltpu.VMEM
    dma = pltpu.SemaphoreType.DMA
    big = (groups, bins, LANES)
    peers = max(pn - 1, 1)
    sm, sh = pl.pallas_call(
        functools.partial(smooth_kernel, n, pn, groups, gw, regimes),
        out_shape=(
            jax.ShapeDtypeStruct((lat, bins), f32),
            jax.ShapeDtypeStruct((bins, pn * lat), bf16),
        ),
        in_specs=[pl.BlockSpec(memory_space=pl.ANY)] * 6,
        out_specs=[pl.BlockSpec(memory_space=pl.ANY)] * 2,
        scratch_shapes=[
            vm((units, bins), bf16),
            vm((bins, units), bf16),
            vm((pn, groups, units, gw), bf16),
            vm((bins, lat), f32),
            vm((groups, peers, bins, gw), bf16),
            vm((groups, peers, bins, gw), bf16),
        ] + [vm(big, f32)] * 12 + [
            vm((bins // LANES, LANES), jnp.int32),
        ] + [vm(rate.shape, f32)] * 3 + [
            vm((bins, LANES), jnp.int32),
            vm((CHUNKS, LANES), jnp.int32),
            vm((groups, 13, CHUNKS, LANES), f32),
            vm((groups, 4, CHUNKS, LANES), f32),
            vm((n, -(-groups * FIXED // 8) * 8, LANES), f32),
            vm((groups, n, 4, LANES), f32),
            vm((groups, n, 8, LANES), f32),
            vm((groups, 4, CHUNKS, LANES), f32),
            vm((groups, bins, gw), f32),
            vm((groups, gw, bins), f32),
            vm((groups, bins, gw), bf16),
            dma((units // TURN,)),
            dma((pn, groups)),
            dma((4,)),
            dma((groups, peers)),
            dma((groups, peers)),
            dma((n,)),
            dma((n,)),
            dma((groups, n)),
            dma((groups, n)),
            dma((groups, peers)),
            dma((groups, peers)),
            dma((groups, 2)),
        ],
        compiler_params=pltpu.CompilerParams(
            collective_id=0, has_side_effects=True, vmem_limit_bytes=61 * 2**20
        ),
        cost_estimate=pl.CostEstimate(
            flops=2 * units * bins * lat * pn, bytes_accessed=2 * units * (bins + lat * pn),
            transcendentals=0,
        ),
        name="smooth",
    )(observations, info_weight, lab, rate, angle, gain)

    tiles = lat // LANES
    predicted, smoothed = pl.pallas_call(
        functools.partial(predict_kernel, tiles),
        out_shape=(
            jax.ShapeDtypeStruct((readout.shape[0], bins), bf16),
            jax.ShapeDtypeStruct((lat, bins), f32),
        ),
        in_specs=[pl.BlockSpec(memory_space=pl.ANY)] * 3,
        out_specs=[pl.BlockSpec(memory_space=pltpu.HBM)] * 2,
        scratch_shapes=[
            vm(readout.shape, bf16),
            vm(sh.shape, bf16),
            vm((readout.shape[0], bins), bf16),
            dma((tiles + 1,)),
            dma((tiles + 1,)),
        ],
        compiler_params=pltpu.CompilerParams(vmem_limit_bytes=61 * 2**20),
        cost_estimate=pl.CostEstimate(
            flops=2 * readout.shape[0] * bins * lat * pn,
            bytes_accessed=2 * readout.shape[0] * (lat * pn + bins) + 8 * bins * lat,
            transcendentals=0,
        ),
        name="predict",
    )(readout, sh, sm)
    return (smoothed, predicted)


def solution(mesh):
    return jax.shard_map(
        body,
        mesh=mesh,
        in_specs=(
            P("panel", "tm"),
            P("panel", None),
            P("panel", None),
            P("tm"),
            P(None, "panel"),
            P(None, "panel"),
            P(None, "panel"),
        ),
        out_specs=(P("panel", "tm"), P("panel", "tm")),
        check_vma=False,
    )
```

```python
import functools

import jax
import jax.numpy as jnp
from jax import lax
from jax.experimental import pallas as pl
from jax.experimental.pallas import tpu as pltpu
from jax.sharding import PartitionSpec as P

LANES = 128
HALF = 64
CHUNKS = 8
TURN = 256
FIXED = 9
MESH = pl.DeviceIdType.MESH


def mul(x, y):
    return x[0] * y[0] - x[1] * y[1], x[0] * y[1] + x[1] * y[0]


def cmul(x, y):
    return x[0] * y[0] + x[1] * y[1], x[0] * y[1] - x[1] * y[0]


def add(x, y):
    return x[0] + y[0], x[1] + y[1]


def smooth_kernel(
    n, pn, groups, gw, regimes,
    obs_hbm, w_hbm, lab_hbm, rate_hbm, angle_hbm, gain_hbm,
    sm_hbm, sh_hbm,
    obs, obs_t, w, own, rs_out, rs_in, xre, xim, are, aim, scl, vre, vim, coef, mre, mim, pre, pim,
    lab_ref, rate_ref, angle_ref, gain_ref, lab, lab_rows, chunk, joint, fixed, moving, enter, bound, smv, smt, shv,
    obs_sem, w_sem, small_sem, rs_send, rs_recv, fx_send, fx_recv, cm_send, cm_recv, ag_send, ag_recv, out_sem,
):
    me = lax.axis_index("tm")
    mp = lax.axis_index("panel")
    units, bins = obs.shape
    lat = own.shape[1]
    steps = bins // CHUNKS
    wide = gw == 2 * LANES

    def panel(s):
        return lax.rem(mp + s, pn)

    turns = units // TURN

    def obs_copy(i):
        rows = pl.ds(pl.multiple_of(i * TURN, TURN), TURN)
        return pltpu.make_async_copy(obs_hbm.at[rows], obs.at[rows], obs_sem.at[i])

    def w_copy(g, s):
        columns = pl.ds(pl.multiple_of(panel(s) * lat + g * gw, LANES), gw)
        return pltpu.make_async_copy(w_hbm.at[:, columns], w.at[s, g], w_sem.at[s, g])

    def load(i, _):
        obs_copy(i).start()
        return 0

    lax.fori_loop(0, turns, load, 0)
    for g in range(groups):
        for s in range(1, pn):
            w_copy(g, s).start()
    for g in range(groups):
        w_copy(g, 0).start()

    small_copies = [
        pltpu.make_async_copy(src, dst, small_sem.at[i])
        for i, (src, dst) in enumerate((
            (lab_hbm, lab_ref), (rate_hbm, rate_ref), (angle_hbm, angle_ref), (gain_hbm, gain_ref)
        ))
    ]
    for copy in small_copies:
        copy.start()

    barrier = pltpu.get_barrier_semaphore()

    for s in range(1, pn):
        pl.semaphore_signal(barrier, inc=1, device_id=(me, panel(s)), device_id_type=MESH)

    def greet(s, _):
        pl.semaphore_signal(
            barrier, inc=1, device_id=(lax.rem(me + s, n), mp), device_id_type=MESH
        )
        return 0

    lax.fori_loop(1, n, greet, 0)

    def rows_of(k):
        return pl.ds(pl.multiple_of(k * CHUNKS, CHUNKS), CHUNKS)

    def spread_labels():
        for c in range(CHUNKS):
            row, first = divmod(c * steps, LANES)
            x = lab_ref[row:row + 1, :]
            lab_rows[c:c + 1, :] = x if first == 0 else pltpu.roll(x, LANES - first, 1)
        x = lab_rows[...]
        for k in range(steps):
            lab[k * CHUNKS:(k + 1) * CHUNKS, :] = jnp.broadcast_to(x[:, k:k + 1], (CHUNKS, LANES))

    def prepare(g):
        lanes = slice(g * LANES, (g + 1) * LANES)
        rate, angle = rate_ref[:, lanes], angle_ref[:, lanes]
        x = 2.0 * rate
        series = 1.0 - x * (1.0 / 8.0)
        for term in range(7, 1, -1):
            series = 1.0 - x * (1.0 / term) * series
        spread = jnp.where(x < 0.25, x * series, 1.0 - jnp.exp(-x))
        mag = jnp.exp(-rate)
        values = (
            mag * jnp.cos(angle), mag * jnp.sin(angle),
            gain_ref[:, lanes] * jnp.sqrt(spread), spread,
        )
        table = [
            [jnp.broadcast_to(v[r:r + 1, :], (CHUNKS, LANES)) for r in range(regimes)]
            for v in values
        ]

        def at(k):
            label = lab[rows_of(k), :]
            which = [label == r for r in range(regimes)]

            def pick(q):
                value = table[q][0]
                for r in range(1, regimes):
                    value = jnp.where(which[r], table[q][r], value)
                return value

            return (pick(0), pick(1)), pick(2), pick(3)

        def keep(k, a, scale, c, p):
            rows = rows_of(k)
            are[g, rows, :], aim[g, rows, :] = a
            scl[g, rows, :], coef[g, rows, :] = scale, c
            pre[g, rows, :], pim[g, rows, :] = p

        def step(k, carry):
            p, q, d = carry
            a, scale, c = at(k)
            v = (c * q[0], -(c * q[1]))
            before = rows_of(k - 1)
            vre[g, before, :], vim[g, before, :] = v
            d = add(d, mul(v, p))
            p, q = mul(a, p), mul(a, q)
            keep(k, a, scale, c, p)
            return p, q, d

        zero = jnp.zeros((CHUNKS, LANES), jnp.float32)
        one = jnp.ones((CHUNKS, LANES), jnp.float32)
        a0, scale0, c0 = at(0)
        keep(0, a0, scale0, c0, a0)
        p, q, d = lax.fori_loop(1, steps, step, (a0, (one, zero), (zero, zero)), unroll=3)
        end = rows_of(steps - 1)
        vre[g, end, :], vim[g, end, :] = zero, zero
        for row, x in zip((0, 1, 4, 5, 8, 9, 10, 11, 12), (*p, q[0], -q[1], *d, *a0, c0)):
            chunk[g, row] = x

    def chunk_row(g, q, c):
        return chunk[g, q, c:c + 1, :]

    def pair_row(g, q, c):
        return chunk_row(g, q, c), chunk_row(g, q + 1, c)

    def chunk_map(g, c):
        return *(pair_row(g, q, c) for q in (0, 4, 8, 10)), chunk_row(g, 12, c)

    def join_fixed(g):
        A, G, D, a0, c0 = chunk_map(g, 0)
        for c in range(1, CHUNKS):
            Ar, Gr, Dr, ar, cr = chunk_map(g, c)
            K = cmul(ar, Dr)
            K = mul(G, (K[0] + cr, K[1]))
            M = mul(G, (ar[0], -ar[1]))
            for row, x in enumerate((*M, *K)):
                joint[g, row, c:c + 1, :] = x
            D = add(D, mul(K, A))
            G = mul(M, Gr)
            A = mul(Ar, A)
        for row, x in enumerate((*A, *G, *D, *a0, c0)):
            fixed[0, g * FIXED + row:g * FIXED + row + 1, :] = x
        last = groups * FIXED
        if g == groups - 1 and last < fixed.shape[1]:
            fixed[0, last:, :] = jnp.zeros((fixed.shape[1] - last, LANES), jnp.float32)

    def turn(i, _):
        obs_copy(i).wait()
        rows = pl.ds(pl.multiple_of(i * TURN, TURN), TURN)
        obs_t[:, rows] = obs[rows, :].T
        return 0

    lax.fori_loop(0, turns, turn, 0)

    def rs_copy(g, s):
        return pltpu.make_async_remote_copy(
            src_ref=rs_out.at[g, s - 1], dst_ref=rs_in.at[g, s - 1],
            send_sem=rs_send.at[g, s - 1], recv_sem=rs_recv.at[g, s - 1],
            device_id=(me, panel(s)), device_id_type=MESH,
        )

    def project(g, s):
        w_copy(g, s).wait()
        return jnp.dot(obs_t[...], w[s, g], preferred_element_type=jnp.float32)

    for g in range(groups):
        for s in range(1, pn):
            rs_out[g, s - 1] = project(g, s).astype(jnp.bfloat16)
            if g == 0:
                if s == 1:
                    pl.semaphore_wait(barrier, n - 1 + pn - 1)
                rs_copy(g, s).start()

    def each_peer(act):
        def go(s, _):
            act(s)
            return 0

        lax.fori_loop(1, n, go, 0)

    def fx_copy(s):
        return pltpu.make_async_remote_copy(
            src_ref=fixed.at[0], dst_ref=fixed.at[s],
            send_sem=fx_send.at[s], recv_sem=fx_recv.at[s],
            device_id=(lax.rem(me + s, n), mp), device_id_type=MESH,
        )

    for copy in small_copies:
        copy.wait()
    spread_labels()
    for g in range(groups):
        prepare(g)
        join_fixed(g)
    each_peer(lambda s: fx_copy(s).start())
    for g in range(groups):
        own[:, g * gw:(g + 1) * gw] = project(g, 0)

    lane = lax.broadcasted_iota(jnp.int32, (bins, LANES), 1)
    low = lane < HALF

    def swap(x):
        return pltpu.roll(x, HALF, 1)

    def gather_info(g):
        for s in range(1, pn):
            rs_copy(g, s).wait_recv()
        parts = []
        for h in range(gw // LANES):
            x = own[:, g * gw + h * LANES:g * gw + (h + 1) * LANES]
            for s in range(1, pn):
                x = x + rs_in[g, s - 1, :, h * LANES:(h + 1) * LANES].astype(jnp.float32)
            parts.append(x)
        if wide:
            xre[g] = jnp.where(low, parts[0], swap(parts[1]))
            xim[g] = jnp.where(low, swap(parts[0]), parts[1])
        else:
            xre[g] = parts[0]
            xim[g] = swap(parts[0])

    def scan(g):
        def step(k, carry):
            m, e = carry
            rows = rows_of(k)
            bin_rows = pl.ds(k, CHUNKS, stride=steps)
            scale = scl[g, rows, :]
            u = (scale * xre[g, bin_rows, :], scale * xim[g, bin_rows, :])
            m = add(mul((are[g, rows, :], aim[g, rows, :]), m), u)
            e = add(e, mul((vre[g, rows, :], vim[g, rows, :]), m))
            mre[g, rows, :], mim[g, rows, :] = m
            return m, e

        zero = jnp.zeros((CHUNKS, LANES), jnp.float32)
        b, e = lax.fori_loop(0, steps, step, ((zero, zero), (zero, zero)), unroll=4)
        chunk[g, 2], chunk[g, 3] = b
        chunk[g, 6], chunk[g, 7] = e

    def local_map(g):
        scan(g)
        B, E = pair_row(g, 2, 0), pair_row(g, 6, 0)
        for c in range(1, CHUNKS):
            M = (joint[g, 0, c:c + 1, :], joint[g, 1, c:c + 1, :])
            K = (joint[g, 2, c:c + 1, :], joint[g, 3, c:c + 1, :])
            E = add(E, add(mul(M, pair_row(g, 6, c)), mul(K, B)))
            B = add(mul(pair_row(g, 0, c), B), pair_row(g, 2, c))
        for row, x in enumerate((*B, *E)):
            moving[g, 0, row:row + 1, :] = x

    def cm_copy(g, s):
        return pltpu.make_async_remote_copy(
            src_ref=moving.at[g, 0], dst_ref=moving.at[g, s],
            send_sem=cm_send.at[g, s], recv_sem=cm_recv.at[g, s],
            device_id=(lax.rem(me + s, n), mp), device_id_type=MESH,
        )

    def boundary(g):
        zero = jnp.zeros((1, LANES), jnp.float32)

        def still(slot, q):
            q = g * FIXED + q
            return fixed[slot, q:q + 1, :], fixed[slot, q + 1:q + 2, :]

        def fresh(slot, q):
            return moving[g, slot, q:q + 1, :], moving[g, slot, q + 1:q + 2, :]

        def put(d, row, value):
            enter[g, d, row:row + 1, :], enter[g, d, row + 1:row + 2, :] = value

        def get(d, row):
            return enter[g, d, row:row + 1, :], enter[g, d, row + 1:row + 2, :]

        def ahead(d, m):
            slot = lax.rem(me - d + n, n)
            put(d, 0, m)
            return add(mul(still(slot, 0), m), fresh(slot, 0))

        last = lax.fori_loop(0, n, ahead, (zero, zero), unroll=4)

        def back(i, s):
            d = n - 1 - i
            slot = lax.rem(me - d + n, n)
            put(d, 2, s)
            m = get(d, 0)
            first = add(add(mul(still(slot, 2), s), fresh(slot, 2)), mul(still(slot, 4), m))
            c = fixed[slot, g * FIXED + 8:g * FIXED + 9, :]
            return add(cmul(still(slot, 6), first), (c * m[0], c * m[1]))

        lax.fori_loop(0, n, back, last, unroll=4)
        m_in, s_in = get(me, 0), get(me, 2)
        return m_in, s_in

    def finish(g):
        m, s = boundary(g)
        entering = []
        for c in range(CHUNKS):
            entering.append(m)
            bound[g, 0, c:c + 1, :], bound[g, 1, c:c + 1, :] = m
            m = add(mul(pair_row(g, 0, c), m), pair_row(g, 2, c))
        for c in reversed(range(CHUNKS)):
            bound[g, 2, c:c + 1, :], bound[g, 3, c:c + 1, :] = s
            _, G, D, a0, c0 = chunk_map(g, c)
            m = entering[c]
            first = add(add(mul(G, s), pair_row(g, 6, c)), mul(D, m))
            s = add(cmul(a0, first), (c0 * m[0], c0 * m[1]))
        m_in = (bound[g, 0], bound[g, 1])
        s_in = (bound[g, 2], bound[g, 3])
        end = pl.ds(steps - 1, CHUNKS, stride=steps)
        xre[g, end, :], xim[g, end, :] = s_in

        def step(i, s):
            k = steps - 2 - i
            rows, after = rows_of(k), rows_of(k + 1)
            a = (are[g, after, :], aim[g, after, :])
            c = coef[g, after, :]
            m = add((mre[g, rows, :], mim[g, rows, :]), mul((pre[g, rows, :], pim[g, rows, :]), m_in))
            s = add(cmul(a, s), (c * m[0], c * m[1]))
            bin_rows = pl.ds(k, CHUNKS, stride=steps)
            xre[g, bin_rows, :], xim[g, bin_rows, :] = s
            return s

        lax.fori_loop(0, steps - 1, step, s_in, unroll=3)
        re, im = xre[g], xim[g]
        parts = [jnp.where(low, re, swap(im))]
        if wide:
            parts.append(jnp.where(low, swap(re), im))
        for h, x in enumerate(parts):
            smv[g, :, h * LANES:(h + 1) * LANES] = x
            shv[g, :, h * LANES:(h + 1) * LANES] = x.astype(jnp.bfloat16)

    def sh_columns(g):
        return pl.ds(pl.multiple_of(mp * lat + g * gw, LANES), gw)

    def ag_copy(g, s):
        return pltpu.make_async_remote_copy(
            src_ref=shv.at[g], dst_ref=sh_hbm.at[:, sh_columns(g)],
            send_sem=ag_send.at[g, s - 1], recv_sem=ag_recv.at[g, s - 1],
            device_id=(me, panel(s)), device_id_type=MESH,
        )

    def sh_copy(g):
        return pltpu.make_async_copy(shv.at[g], sh_hbm.at[:, sh_columns(g)], out_sem.at[g, 0])

    def sm_copy(g):
        return pltpu.make_async_copy(smt.at[g], sm_hbm.at[pl.ds(g * gw, gw)], out_sem.at[g, 1])

    def turn_out(g):
        for h in range(gw // LANES):
            lanes = slice(h * LANES, (h + 1) * LANES)
            smt[g, lanes, :] = smv[g, :, lanes].T
        sm_copy(g).start()

    for g in range(groups):
        for s in range(1, pn):
            rs_copy(g, s).wait_send()
        if g < groups - 1:
            for s in range(1, pn):
                rs_copy(g + 1, s).start()
        gather_info(g)
        local_map(g)
        each_peer(lambda s: cm_copy(g, s).start())
        if g == 0:
            each_peer(lambda s: fx_copy(s).wait_recv())
        else:
            turn_out(g - 1)
        each_peer(lambda s: cm_copy(g, s).wait_recv())
        finish(g)
        for s in range(1, pn):
            ag_copy(g, s).start()
        sh_copy(g).start()
    turn_out(groups - 1)
    each_peer(lambda s: fx_copy(s).wait_send())
    for g in range(groups):
        each_peer(lambda s: cm_copy(g, s).wait_send())
        sh_copy(g).wait()
        sm_copy(g).wait()
        for s in range(1, pn):
            ag_copy(g, s).wait()


def predict_kernel(
    tiles, readout_hbm, sh_hbm, sm_hbm, predicted, smoothed, readout, sh, sm, out, in_sems, sems
):
    rows = readout.shape[0] // tiles
    loads, copies = [], []

    def begin(into, src, dst, sem):
        into.append(pltpu.make_async_copy(src, dst, sem))
        into[-1].start()

    begin(loads, sh_hbm, sh, in_sems.at[tiles])
    for i in range(tiles):
        part = pl.ds(i * rows, rows)
        begin(loads, readout_hbm.at[part], readout.at[part], in_sems.at[i])
    begin(loads, sm_hbm, sm, in_sems.at[tiles + 1])
    loads[0].wait()
    for i in range(tiles):
        part = pl.ds(i * rows, rows)
        loads[i + 1].wait()
        out[part, :] = lax.dot_general(
            readout[part, :], sh[...],
            (((1,), (1,)), ((), ())), preferred_element_type=jnp.float32,
        ).astype(jnp.bfloat16)
        begin(copies, out.at[part], predicted.at[part], sems.at[i])
        if i == 0:
            loads[-1].wait()
            begin(copies, sm, smoothed, sems.at[tiles])
    for copy in copies:
        copy.wait()


def body(observations, info_weight, readout, labels, rate, angle, gain):
    units, bins = observations.shape
    n, pn = lax.axis_size("tm"), lax.axis_size("panel")
    lat = info_weight.shape[1] // pn
    gw = 2 * LANES if lat % (2 * LANES) == 0 else LANES
    groups = lat // gw
    regimes = rate.shape[0]

    short = groups * LANES - rate.shape[1]
    if short:
        rate, angle, gain = (
            jnp.pad(x, ((0, 0), (0, short)), constant_values=0.25) for x in (rate, angle, gain)
        )
    lab = labels.reshape(bins // LANES, LANES)

    f32, bf16 = jnp.float32, jnp.bfloat16
    vm = pltpu.VMEM
    dma = pltpu.SemaphoreType.DMA
    big = (groups, bins, LANES)
    peers = max(pn - 1, 1)
    sm, sh = pl.pallas_call(
        functools.partial(smooth_kernel, n, pn, groups, gw, regimes),
        out_shape=(
            jax.ShapeDtypeStruct((lat, bins), f32),
            jax.ShapeDtypeStruct((bins, pn * lat), bf16),
        ),
        in_specs=[pl.BlockSpec(memory_space=pl.ANY)] * 6,
        out_specs=[pl.BlockSpec(memory_space=pl.ANY)] * 2,
        scratch_shapes=[
            vm((units, bins), bf16),
            vm((bins, units), bf16),
            vm((pn, groups, units, gw), bf16),
            vm((bins, lat), f32),
            vm((groups, peers, bins, gw), bf16),
            vm((groups, peers, bins, gw), bf16),
        ] + [vm(big, f32)] * 12 + [
            vm((bins // LANES, LANES), jnp.int32),
        ] + [vm(rate.shape, f32)] * 3 + [
            vm((bins, LANES), jnp.int32),
            vm((CHUNKS, LANES), jnp.int32),
            vm((groups, 13, CHUNKS, LANES), f32),
            vm((groups, 4, CHUNKS, LANES), f32),
            vm((n, -(-groups * FIXED // 8) * 8, LANES), f32),
            vm((groups, n, 4, LANES), f32),
            vm((groups, n, 8, LANES), f32),
            vm((groups, 4, CHUNKS, LANES), f32),
            vm((groups, bins, gw), f32),
            vm((groups, gw, bins), f32),
            vm((groups, bins, gw), bf16),
            dma((units // TURN,)),
            dma((pn, groups)),
            dma((4,)),
            dma((groups, peers)),
            dma((groups, peers)),
            dma((n,)),
            dma((n,)),
            dma((groups, n)),
            dma((groups, n)),
            dma((groups, peers)),
            dma((groups, peers)),
            dma((groups, 2)),
        ],
        compiler_params=pltpu.CompilerParams(
            collective_id=0, has_side_effects=True, vmem_limit_bytes=61 * 2**20
        ),
        cost_estimate=pl.CostEstimate(
            flops=2 * units * bins * lat * pn, bytes_accessed=2 * units * (bins + lat * pn),
            transcendentals=0,
        ),
        name="smooth",
    )(observations, info_weight, lab, rate, angle, gain)

    tiles = lat // LANES
    predicted, smoothed = pl.pallas_call(
        functools.partial(predict_kernel, tiles),
        out_shape=(
            jax.ShapeDtypeStruct((readout.shape[0], bins), bf16),
            jax.ShapeDtypeStruct((lat, bins), f32),
        ),
        in_specs=[pl.BlockSpec(memory_space=pl.ANY)] * 3,
        out_specs=[pl.BlockSpec(memory_space=pltpu.HBM)] * 2,
        scratch_shapes=[
            vm(readout.shape, bf16),
            vm(sh.shape, bf16),
            vm(sm.shape, f32),
            vm((readout.shape[0], bins), bf16),
            dma((tiles + 2,)),
            dma((tiles + 1,)),
        ],
        compiler_params=pltpu.CompilerParams(vmem_limit_bytes=61 * 2**20),
        cost_estimate=pl.CostEstimate(
            flops=2 * readout.shape[0] * bins * lat * pn,
            bytes_accessed=2 * readout.shape[0] * (lat * pn + bins) + 8 * bins * lat,
            transcendentals=0,
        ),
        name="predict",
    )(readout, sh, sm)
    return (smoothed, predicted)


def solution(mesh):
    return jax.shard_map(
        body,
        mesh=mesh,
        in_specs=(
            P("panel", "tm"),
            P("panel", None),
            P("panel", None),
            P("tm"),
            P(None, "panel"),
            P(None, "panel"),
            P(None, "panel"),
        ),
        out_specs=(P("panel", "tm"), P("panel", "tm")),
        check_vma=False,
    )
```

```python
import functools

import jax
import jax.numpy as jnp
from jax import lax
from jax.experimental import pallas as pl
from jax.experimental.pallas import tpu as pltpu
from jax.sharding import PartitionSpec as P

LANES = 128
HALF = 64
CHUNKS = 8
TURN = 256
FIXED = 9
MESH = pl.DeviceIdType.MESH


def mul(x, y):
    return x[0] * y[0] - x[1] * y[1], x[0] * y[1] + x[1] * y[0]


def cmul(x, y):
    return x[0] * y[0] + x[1] * y[1], x[0] * y[1] - x[1] * y[0]


def add(x, y):
    return x[0] + y[0], x[1] + y[1]


def smooth_kernel(
    n, pn, groups, gw, regimes,
    obs_hbm, w_hbm, lab_hbm, rate_hbm, angle_hbm, gain_hbm,
    sm_hbm, sh_hbm,
    obs, obs_t, w, own, rs_out, rs_in, xre, xim, are, aim, scl, vre, vim, coef, mre, mim, pre, pim,
    lab_ref, rate_ref, angle_ref, gain_ref, lab, lab_rows, chunk, joint, fixed, moving, enter, bound, smv, smt, shv,
    obs_sem, w_sem, small_sem, rs_send, rs_recv, fx_send, fx_recv, cm_send, cm_recv, ag_send, ag_recv, out_sem,
):
    me = lax.axis_index("tm")
    mp = lax.axis_index("panel")
    units, bins = obs.shape
    lat = own.shape[1]
    steps = bins // CHUNKS
    wide = gw == 2 * LANES

    def panel(s):
        return lax.rem(mp + s, pn)

    turns = units // TURN

    def obs_copy(i):
        rows = pl.ds(pl.multiple_of(i * TURN, TURN), TURN)
        return pltpu.make_async_copy(obs_hbm.at[rows], obs.at[rows], obs_sem.at[i])

    def w_copy(g, s):
        columns = pl.ds(pl.multiple_of(panel(s) * lat + g * gw, LANES), gw)
        return pltpu.make_async_copy(w_hbm.at[:, columns], w.at[s, g], w_sem.at[s, g])

    def load(i, _):
        obs_copy(i).start()
        return 0

    lax.fori_loop(0, turns, load, 0)
    for g in range(groups):
        for s in range(1, pn):
            w_copy(g, s).start()
    for g in range(groups):
        w_copy(g, 0).start()

    small_copies = [
        pltpu.make_async_copy(src, dst, small_sem.at[i])
        for i, (src, dst) in enumerate((
            (lab_hbm, lab_ref), (rate_hbm, rate_ref), (angle_hbm, angle_ref), (gain_hbm, gain_ref)
        ))
    ]
    for copy in small_copies:
        copy.start()

    barrier = pltpu.get_barrier_semaphore()

    for s in range(1, pn):
        pl.semaphore_signal(barrier, inc=1, device_id=(me, panel(s)), device_id_type=MESH)

    def greet(s, _):
        pl.semaphore_signal(
            barrier, inc=1, device_id=(lax.rem(me + s, n), mp), device_id_type=MESH
        )
        return 0

    lax.fori_loop(1, n, greet, 0)

    def rows_of(k):
        return pl.ds(pl.multiple_of(k * CHUNKS, CHUNKS), CHUNKS)

    def spread_labels():
        for c in range(CHUNKS):
            row, first = divmod(c * steps, LANES)
            x = lab_ref[row:row + 1, :]
            lab_rows[c:c + 1, :] = x if first == 0 else pltpu.roll(x, LANES - first, 1)
        x = lab_rows[...]
        for k in range(steps):
            lab[k * CHUNKS:(k + 1) * CHUNKS, :] = jnp.broadcast_to(x[:, k:k + 1], (CHUNKS, LANES))

    def prepare(g):
        lanes = slice(g * LANES, (g + 1) * LANES)
        rate, angle = rate_ref[:, lanes], angle_ref[:, lanes]
        x = 2.0 * rate
        series = 1.0 - x * (1.0 / 8.0)
        for term in range(7, 1, -1):
            series = 1.0 - x * (1.0 / term) * series
        spread = jnp.where(x < 0.25, x * series, 1.0 - jnp.exp(-x))
        mag = jnp.exp(-rate)
        values = (
            mag * jnp.cos(angle), mag * jnp.sin(angle),
            gain_ref[:, lanes] * jnp.sqrt(spread), spread,
        )
        table = [
            [jnp.broadcast_to(v[r:r + 1, :], (CHUNKS, LANES)) for r in range(regimes)]
            for v in values
        ]

        def at(k):
            label = lab[rows_of(k), :]
            which = [label == r for r in range(regimes)]

            def pick(q):
                value = table[q][0]
                for r in range(1, regimes):
                    value = jnp.where(which[r], table[q][r], value)
                return value

            return (pick(0), pick(1)), pick(2), pick(3)

        def keep(k, a, scale, c, p):
            rows = rows_of(k)
            are[g, rows, :], aim[g, rows, :] = a
            scl[g, rows, :], coef[g, rows, :] = scale, c
            pre[g, rows, :], pim[g, rows, :] = p

        def step(k, carry):
            p, q, d = carry
            a, scale, c = at(k)
            v = (c * q[0], -(c * q[1]))
            before = rows_of(k - 1)
            vre[g, before, :], vim[g, before, :] = v
            d = add(d, mul(v, p))
            p, q = mul(a, p), mul(a, q)
            keep(k, a, scale, c, p)
            return p, q, d

        zero = jnp.zeros((CHUNKS, LANES), jnp.float32)
        one = jnp.ones((CHUNKS, LANES), jnp.float32)
        a0, scale0, c0 = at(0)
        keep(0, a0, scale0, c0, a0)
        p, q, d = lax.fori_loop(1, steps, step, (a0, (one, zero), (zero, zero)), unroll=3)
        end = rows_of(steps - 1)
        vre[g, end, :], vim[g, end, :] = zero, zero
        for row, x in zip((0, 1, 4, 5, 8, 9, 10, 11, 12), (*p, q[0], -q[1], *d, *a0, c0)):
            chunk[g, row] = x

    def chunk_row(g, q, c):
        return chunk[g, q, c:c + 1, :]

    def pair_row(g, q, c):
        return chunk_row(g, q, c), chunk_row(g, q + 1, c)

    def chunk_map(g, c):
        return *(pair_row(g, q, c) for q in (0, 4, 8, 10)), chunk_row(g, 12, c)

    def join_fixed(g):
        A, G, D, a0, c0 = chunk_map(g, 0)
        for c in range(1, CHUNKS):
            Ar, Gr, Dr, ar, cr = chunk_map(g, c)
            K = cmul(ar, Dr)
            K = mul(G, (K[0] + cr, K[1]))
            M = mul(G, (ar[0], -ar[1]))
            for row, x in enumerate((*M, *K)):
                joint[g, row, c:c + 1, :] = x
            D = add(D, mul(K, A))
            G = mul(M, Gr)
            A = mul(Ar, A)
        for row, x in enumerate((*A, *G, *D, *a0, c0)):
            fixed[0, g * FIXED + row:g * FIXED + row + 1, :] = x
        last = groups * FIXED
        if g == groups - 1 and last < fixed.shape[1]:
            fixed[0, last:, :] = jnp.zeros((fixed.shape[1] - last, LANES), jnp.float32)

    def turn(i, _):
        obs_copy(i).wait()
        rows = pl.ds(pl.multiple_of(i * TURN, TURN), TURN)
        obs_t[:, rows] = obs[rows, :].T
        return 0

    lax.fori_loop(0, turns, turn, 0)

    def rs_copy(g, s):
        return pltpu.make_async_remote_copy(
            src_ref=rs_out.at[g, s - 1], dst_ref=rs_in.at[g, s - 1],
            send_sem=rs_send.at[g, s - 1], recv_sem=rs_recv.at[g, s - 1],
            device_id=(me, panel(s)), device_id_type=MESH,
        )

    def project(g, s):
        w_copy(g, s).wait()
        return jnp.dot(obs_t[...], w[s, g], preferred_element_type=jnp.float32)

    for g in range(groups):
        for s in range(1, pn):
            rs_out[g, s - 1] = project(g, s).astype(jnp.bfloat16)
            if g == 0:
                if s == 1:
                    pl.semaphore_wait(barrier, n - 1 + pn - 1)
                rs_copy(g, s).start()

    def each_peer(act):
        def go(s, _):
            act(s)
            return 0

        lax.fori_loop(1, n, go, 0)

    def fx_copy(s):
        return pltpu.make_async_remote_copy(
            src_ref=fixed.at[0], dst_ref=fixed.at[s],
            send_sem=fx_send.at[s], recv_sem=fx_recv.at[s],
            device_id=(lax.rem(me + s, n), mp), device_id_type=MESH,
        )

    for copy in small_copies:
        copy.wait()
    spread_labels()
    for g in range(groups):
        prepare(g)
        join_fixed(g)
    each_peer(lambda s: fx_copy(s).start())
    for g in range(groups):
        own[:, g * gw:(g + 1) * gw] = project(g, 0)

    lane = lax.broadcasted_iota(jnp.int32, (bins, LANES), 1)
    low = lane < HALF

    def swap(x):
        return pltpu.roll(x, HALF, 1)

    def gather_info(g):
        for s in range(1, pn):
            rs_copy(g, s).wait_recv()
        parts = []
        for h in range(gw // LANES):
            x = own[:, g * gw + h * LANES:g * gw + (h + 1) * LANES]
            for s in range(1, pn):
                x = x + rs_in[g, s - 1, :, h * LANES:(h + 1) * LANES].astype(jnp.float32)
            parts.append(x)
        if wide:
            xre[g] = jnp.where(low, parts[0], swap(parts[1]))
            xim[g] = jnp.where(low, swap(parts[0]), parts[1])
        else:
            xre[g] = parts[0]
            xim[g] = swap(parts[0])

    def scan(g):
        def step(k, carry):
            m, e = carry
            rows = rows_of(k)
            bin_rows = pl.ds(k, CHUNKS, stride=steps)
            scale = scl[g, rows, :]
            u = (scale * xre[g, bin_rows, :], scale * xim[g, bin_rows, :])
            m = add(mul((are[g, rows, :], aim[g, rows, :]), m), u)
            e = add(e, mul((vre[g, rows, :], vim[g, rows, :]), m))
            mre[g, rows, :], mim[g, rows, :] = m
            return m, e

        zero = jnp.zeros((CHUNKS, LANES), jnp.float32)
        b, e = lax.fori_loop(0, steps, step, ((zero, zero), (zero, zero)), unroll=4)
        chunk[g, 2], chunk[g, 3] = b
        chunk[g, 6], chunk[g, 7] = e

    def local_map(g):
        scan(g)
        B, E = pair_row(g, 2, 0), pair_row(g, 6, 0)
        for c in range(1, CHUNKS):
            M = (joint[g, 0, c:c + 1, :], joint[g, 1, c:c + 1, :])
            K = (joint[g, 2, c:c + 1, :], joint[g, 3, c:c + 1, :])
            E = add(E, add(mul(M, pair_row(g, 6, c)), mul(K, B)))
            B = add(mul(pair_row(g, 0, c), B), pair_row(g, 2, c))
        for row, x in enumerate((*B, *E)):
            moving[g, 0, row:row + 1, :] = x

    def cm_copy(g, s):
        return pltpu.make_async_remote_copy(
            src_ref=moving.at[g, 0], dst_ref=moving.at[g, s],
            send_sem=cm_send.at[g, s], recv_sem=cm_recv.at[g, s],
            device_id=(lax.rem(me + s, n), mp), device_id_type=MESH,
        )

    def boundary(g):
        zero = jnp.zeros((1, LANES), jnp.float32)

        def still(slot, q):
            q = g * FIXED + q
            return fixed[slot, q:q + 1, :], fixed[slot, q + 1:q + 2, :]

        def fresh(slot, q):
            return moving[g, slot, q:q + 1, :], moving[g, slot, q + 1:q + 2, :]

        def put(d, row, value):
            enter[g, d, row:row + 1, :], enter[g, d, row + 1:row + 2, :] = value

        def get(d, row):
            return enter[g, d, row:row + 1, :], enter[g, d, row + 1:row + 2, :]

        def ahead(d, m):
            slot = lax.rem(me - d + n, n)
            put(d, 0, m)
            return add(mul(still(slot, 0), m), fresh(slot, 0))

        last = lax.fori_loop(0, n, ahead, (zero, zero), unroll=4)

        def back(i, s):
            d = n - 1 - i
            slot = lax.rem(me - d + n, n)
            put(d, 2, s)
            m = get(d, 0)
            first = add(add(mul(still(slot, 2), s), fresh(slot, 2)), mul(still(slot, 4), m))
            c = fixed[slot, g * FIXED + 8:g * FIXED + 9, :]
            return add(cmul(still(slot, 6), first), (c * m[0], c * m[1]))

        lax.fori_loop(0, n, back, last, unroll=4)
        m_in, s_in = get(me, 0), get(me, 2)
        return m_in, s_in

    def finish(g):
        m, s = boundary(g)
        entering = []
        for c in range(CHUNKS):
            entering.append(m)
            bound[g, 0, c:c + 1, :], bound[g, 1, c:c + 1, :] = m
            m = add(mul(pair_row(g, 0, c), m), pair_row(g, 2, c))
        for c in reversed(range(CHUNKS)):
            bound[g, 2, c:c + 1, :], bound[g, 3, c:c + 1, :] = s
            _, G, D, a0, c0 = chunk_map(g, c)
            m = entering[c]
            first = add(add(mul(G, s), pair_row(g, 6, c)), mul(D, m))
            s = add(cmul(a0, first), (c0 * m[0], c0 * m[1]))
        m_in = (bound[g, 0], bound[g, 1])
        s_in = (bound[g, 2], bound[g, 3])
        end = pl.ds(steps - 1, CHUNKS, stride=steps)
        xre[g, end, :], xim[g, end, :] = s_in

        def step(i, s):
            k = steps - 2 - i
            rows, after = rows_of(k), rows_of(k + 1)
            a = (are[g, after, :], aim[g, after, :])
            c = coef[g, after, :]
            m = add((mre[g, rows, :], mim[g, rows, :]), mul((pre[g, rows, :], pim[g, rows, :]), m_in))
            s = add(cmul(a, s), (c * m[0], c * m[1]))
            bin_rows = pl.ds(k, CHUNKS, stride=steps)
            xre[g, bin_rows, :], xim[g, bin_rows, :] = s
            return s

        lax.fori_loop(0, steps - 1, step, s_in, unroll=3)
        re, im = xre[g], xim[g]
        parts = [jnp.where(low, re, swap(im))]
        if wide:
            parts.append(jnp.where(low, swap(re), im))
        for h, x in enumerate(parts):
            smv[g, :, h * LANES:(h + 1) * LANES] = x
            shv[g, :, h * LANES:(h + 1) * LANES] = x.astype(jnp.bfloat16)

    def sh_columns(g):
        return pl.ds(pl.multiple_of(mp * lat + g * gw, LANES), gw)

    def ag_copy(g, s):
        return pltpu.make_async_remote_copy(
            src_ref=shv.at[g], dst_ref=sh_hbm.at[:, sh_columns(g)],
            send_sem=ag_send.at[g, s - 1], recv_sem=ag_recv.at[g, s - 1],
            device_id=(me, panel(s)), device_id_type=MESH,
        )

    def sh_copy(g):
        return pltpu.make_async_copy(shv.at[g], sh_hbm.at[:, sh_columns(g)], out_sem.at[g, 0])

    def sm_copy(g):
        return pltpu.make_async_copy(smt.at[g], sm_hbm.at[pl.ds(g * gw, gw)], out_sem.at[g, 1])

    def turn_out(g):
        for h in range(gw // LANES):
            lanes = slice(h * LANES, (h + 1) * LANES)
            smt[g, lanes, :] = smv[g, :, lanes].T
        sm_copy(g).start()

    for g in range(groups):
        for s in range(1, pn):
            rs_copy(g, s).wait_send()
        if g < groups - 1:
            for s in range(1, pn):
                rs_copy(g + 1, s).start()
        gather_info(g)
        local_map(g)
        each_peer(lambda s: cm_copy(g, s).start())
        if g == 0:
            each_peer(lambda s: fx_copy(s).wait_recv())
        else:
            turn_out(g - 1)
        each_peer(lambda s: cm_copy(g, s).wait_recv())
        finish(g)
        for s in range(1, pn):
            ag_copy(g, s).start()
        sh_copy(g).start()
    turn_out(groups - 1)
    each_peer(lambda s: fx_copy(s).wait_send())
    for g in range(groups):
        each_peer(lambda s: cm_copy(g, s).wait_send())
        sh_copy(g).wait()
        sm_copy(g).wait()
        for s in range(1, pn):
            ag_copy(g, s).wait()


def predict_kernel(
    tiles, readout_hbm, sh_hbm, sm_hbm, predicted, smoothed, readout, sh, sm, out, in_sems, sems
):
    rows = readout.shape[0] // tiles
    loads, copies = [], []

    def begin(into, src, dst, sem):
        into.append(pltpu.make_async_copy(src, dst, sem))
        into[-1].start()

    def fetch(i):
        part = pl.ds(i * rows, rows)
        begin(loads, readout_hbm.at[part], readout.at[part], in_sems.at[i])

    begin(loads, sh_hbm, sh, in_sems.at[tiles])
    fetch(0)
    loads[0].wait()
    loads[1].wait()
    for i in range(1, tiles):
        fetch(i)
    begin(loads, sm_hbm, sm, in_sems.at[tiles + 1])
    for i in range(tiles):
        part = pl.ds(i * rows, rows)
        if i:
            loads[i + 1].wait()
        out[part, :] = lax.dot_general(
            readout[part, :], sh[...],
            (((1,), (1,)), ((), ())), preferred_element_type=jnp.float32,
        ).astype(jnp.bfloat16)
        begin(copies, out.at[part], predicted.at[part], sems.at[i])
        if i == tiles // 2:
            loads[-1].wait()
            begin(copies, sm, smoothed, sems.at[tiles])
    for copy in copies:
        copy.wait()


def body(observations, info_weight, readout, labels, rate, angle, gain):
    units, bins = observations.shape
    n, pn = lax.axis_size("tm"), lax.axis_size("panel")
    lat = info_weight.shape[1] // pn
    gw = 2 * LANES if lat % (2 * LANES) == 0 else LANES
    groups = lat // gw
    regimes = rate.shape[0]

    short = groups * LANES - rate.shape[1]
    if short:
        rate, angle, gain = (
            jnp.pad(x, ((0, 0), (0, short)), constant_values=0.25) for x in (rate, angle, gain)
        )
    lab = labels.reshape(bins // LANES, LANES)

    f32, bf16 = jnp.float32, jnp.bfloat16
    vm = pltpu.VMEM
    dma = pltpu.SemaphoreType.DMA
    big = (groups, bins, LANES)
    peers = max(pn - 1, 1)
    sm, sh = pl.pallas_call(
        functools.partial(smooth_kernel, n, pn, groups, gw, regimes),
        out_shape=(
            jax.ShapeDtypeStruct((lat, bins), f32),
            jax.ShapeDtypeStruct((bins, pn * lat), bf16),
        ),
        in_specs=[pl.BlockSpec(memory_space=pl.ANY)] * 6,
        out_specs=[pl.BlockSpec(memory_space=pl.ANY)] * 2,
        scratch_shapes=[
            vm((units, bins), bf16),
            vm((bins, units), bf16),
            vm((pn, groups, units, gw), bf16),
            vm((bins, lat), f32),
            vm((groups, peers, bins, gw), bf16),
            vm((groups, peers, bins, gw), bf16),
        ] + [vm(big, f32)] * 12 + [
            vm((bins // LANES, LANES), jnp.int32),
        ] + [vm(rate.shape, f32)] * 3 + [
            vm((bins, LANES), jnp.int32),
            vm((CHUNKS, LANES), jnp.int32),
            vm((groups, 13, CHUNKS, LANES), f32),
            vm((groups, 4, CHUNKS, LANES), f32),
            vm((n, -(-groups * FIXED // 8) * 8, LANES), f32),
            vm((groups, n, 4, LANES), f32),
            vm((groups, n, 8, LANES), f32),
            vm((groups, 4, CHUNKS, LANES), f32),
            vm((groups, bins, gw), f32),
            vm((groups, gw, bins), f32),
            vm((groups, bins, gw), bf16),
            dma((units // TURN,)),
            dma((pn, groups)),
            dma((4,)),
            dma((groups, peers)),
            dma((groups, peers)),
            dma((n,)),
            dma((n,)),
            dma((groups, n)),
            dma((groups, n)),
            dma((groups, peers)),
            dma((groups, peers)),
            dma((groups, 2)),
        ],
        compiler_params=pltpu.CompilerParams(
            collective_id=0, has_side_effects=True, vmem_limit_bytes=61 * 2**20
        ),
        cost_estimate=pl.CostEstimate(
            flops=2 * units * bins * lat * pn, bytes_accessed=2 * units * (bins + lat * pn),
            transcendentals=0,
        ),
        name="smooth",
    )(observations, info_weight, lab, rate, angle, gain)

    tiles = lat // LANES
    predicted, smoothed = pl.pallas_call(
        functools.partial(predict_kernel, tiles),
        out_shape=(
            jax.ShapeDtypeStruct((readout.shape[0], bins), bf16),
            jax.ShapeDtypeStruct((lat, bins), f32),
        ),
        in_specs=[pl.BlockSpec(memory_space=pl.ANY)] * 3,
        out_specs=[pl.BlockSpec(memory_space=pltpu.HBM)] * 2,
        scratch_shapes=[
            vm(readout.shape, bf16),
            vm(sh.shape, bf16),
            vm(sm.shape, f32),
            vm((readout.shape[0], bins), bf16),
            dma((tiles + 2,)),
            dma((tiles + 1,)),
        ],
        compiler_params=pltpu.CompilerParams(vmem_limit_bytes=61 * 2**20),
        cost_estimate=pl.CostEstimate(
            flops=2 * readout.shape[0] * bins * lat * pn,
            bytes_accessed=2 * readout.shape[0] * (lat * pn + bins) + 8 * bins * lat,
            transcendentals=0,
        ),
        name="predict",
    )(readout, sh, sm)
    return (smoothed, predicted)


def solution(mesh):
    return jax.shard_map(
        body,
        mesh=mesh,
        in_specs=(
            P("panel", "tm"),
            P("panel", None),
            P("panel", None),
            P("tm"),
            P(None, "panel"),
            P(None, "panel"),
            P(None, "panel"),
        ),
        out_specs=(P("panel", "tm"), P("panel", "tm")),
        check_vma=False,
    )
```
